512 devices in a mesh: dp: 8 (over z_lo, core), context: 64 (over y, x, z_hi).
Axes of the slice: x: 4, y: 4, z: 16 (z_hi: 4, z_lo: 4; z = z_hi * 4 + z_lo), core: 2. Of those that a mesh axis runs over, the one named last changes fastest.
Arguments:
- value: bfloat16 [1, 4096, 8192], P(None, 'dp', 'context'), may hold values from -6 to 6
- key_one: bfloat16 [1, 4096, 8192], P(None, 'dp', 'context'), may hold values from -6 to 6
- gate_one: bfloat16 [1, 4096, 8192], P(None, 'dp', 'context'), may hold values from -6 to 6
- conv_one: bfloat16 [1, 4096, 8192], P(None, 'dp', 'context'), may hold values from -6 to 6
- key_two: bfloat16 [1, 4096, 8192], P(None, 'dp', 'context'), may hold values from -6 to 6
- gate_two: bfloat16 [1, 4096, 8192], P(None, 'dp', 'context'), may hold values from -6 to 6
- conv_two: bfloat16 [1, 4096, 8192], P(None, 'dp', 'context'), may hold values from -6 to 6
- grad_out: bfloat16 [1, 4096, 8192], P(None, 'dp', 'context'), may hold values from -16 to 16
- residues_one: float32 [4096, 16], P('dp'), may hold values from -3 to 3
- log_rate_one: float32 [4096, 16], P('dp'), may hold values from -16 to -3
- residues_two: float32 [4096, 16], P('dp'), may hold values from -3 to 3
- log_rate_two: float32 [4096, 16], P('dp'), may hold values from -16 to -3
Outputs:
- grad_value: bfloat16 [1, 4096, 8192], P(None, 'dp', 'context')
- grad_key_one: bfloat16 [1, 4096, 8192], P(None, 'dp', 'context')
- grad_gate_one: bfloat16 [1, 4096, 8192], P(None, 'dp', 'context')
- grad_key_two: bfloat16 [1, 4096, 8192], P(None, 'dp', 'context')
- grad_gate_two: bfloat16 [1, 4096, 8192], P(None, 'dp', 'context')
- grad_residues_one: float32 [4096, 16], P('dp')
- grad_log_rate_one: float32 [4096, 16], P('dp')
- grad_residues_two: float32 [4096, 16], P('dp')
- grad_log_rate_two: float32 [4096, 16], P('dp')
The draws below stay inside these ranges and needn't reach their ends.
All inputs are finite; a program needn't handle non-finite values.
Results may differ from the reference program's by a relative error of at most 0.0022.
Values sent between devices are 32-bit elements; how exact they have to be, the bound alone decides.
A program may use at most 128 MiB of HBM per device.

```python
import math
import jax
import jax.numpy as jnp
from jax import lax

CH = 4096
ORDER = 16
LOC = 128
BATCH = 1
LENGTH = 8192


def decay_logs(key, first, second):
    pick = jax.random.uniform(jax.random.fold_in(key, 1), (CH, ORDER))
    spread = jax.random.uniform(jax.random.fold_in(key, 2), (CH, ORDER))
    slow = jnp.log(0.2 / LENGTH) + spread * jnp.log(10.0)
    middle = jnp.log(1.0 / LOC) + spread * jnp.log(4.0)
    quick = jnp.log(1.0 / 50.0) + spread * jnp.log(50.0 / 30.0)
    return jnp.where(pick < first, slow, jnp.where(pick < second, middle, quick)).astype(jnp.float32)


def draw_log_rate_one(key, part):
    key = jax.random.fold_in(key, 3)
    return decay_logs(key, 0.5, 0.75)


def draw_log_rate_two(key, part):
    key = jax.random.fold_in(key, 5)
    return decay_logs(key, 0.5, 0.75)


def draw_grad_out(key, part):
    key = jax.random.fold_in(key, 11)
    row_ramp = 1.0 + 2.0 * jnp.arange(BATCH).astype(jnp.float32) / max(BATCH - 1, 1)
    pos_ramp = 1.0 + 2.0 * jnp.arange(LENGTH).astype(jnp.float32) / (LENGTH - 1)
    base = jnp.clip(jax.random.normal(key, (BATCH, CH, LENGTH)), -4.0, 4.0)
    values = base * row_ramp[:, None, None] * pos_ramp[None, None, :] / 3.0
    return values.astype(jnp.bfloat16)


def levels(rng, shape, cuts, least, high):
    loudness, own = 1.0, jax.random.fold_in(rng, 6)
    for position, blocks in cuts:
        heights = jnp.exp(jax.random.uniform(jax.random.fold_in(own, position), (blocks,), jnp.float32, least / len(cuts), high / len(cuts)))
        loudness = loudness * jnp.repeat(heights, shape[position] // blocks).reshape([-1 if axis == position else 1 for axis in range(len(shape))])
    return loudness


def bell_draw(rng, shape, width, reach, shards=(), kind=jnp.bfloat16):
    loudness = levels(rng, shape, shards, -0.22, 0.18) if shards else 1.0
    array = jax.random.normal(rng, shape, jnp.float32) * width * loudness
    return jnp.minimum(jnp.maximum(array, -reach), reach).astype(kind)


def setup_inputs(seed: int = 0) -> dict:
    arg_keys = jax.random.split(jax.random.key(seed), 13)
    return {
        "value": bell_draw(arg_keys[0], (BATCH, CH, LENGTH), 1.0, 6.0, ((1, 8), (2, 64))),
        "key_one": bell_draw(arg_keys[1], (BATCH, CH, LENGTH), 1.0, 6.0, ((1, 8), (2, 64))),
        "gate_one": bell_draw(arg_keys[2], (BATCH, CH, LENGTH), 1.0, 6.0, ((1, 8), (2, 64))),
        "conv_one": bell_draw(arg_keys[3], (BATCH, CH, LENGTH), 1.0, 6.0, ((1, 8), (2, 64))),
        "key_two": bell_draw(arg_keys[4], (BATCH, CH, LENGTH), 1.0, 6.0, ((1, 8), (2, 64))),
        "gate_two": bell_draw(arg_keys[5], (BATCH, CH, LENGTH), 1.0, 6.0, ((1, 8), (2, 64))),
        "conv_two": bell_draw(arg_keys[6], (BATCH, CH, LENGTH), 1.0, 6.0, ((1, 8), (2, 64))),
        "grad_out": draw_grad_out(jax.random.fold_in(arg_keys[12], 71), 0),
        "residues_one": bell_draw(arg_keys[8], (CH, ORDER), 0.3, 3.0, ((0, 8),), jnp.float32),
        "log_rate_one": draw_log_rate_one(jax.random.fold_in(arg_keys[12], 71), 0),
        "residues_two": bell_draw(arg_keys[10], (CH, ORDER), 0.3, 3.0, ((0, 8),), jnp.float32),
        "log_rate_two": draw_log_rate_two(jax.random.fold_in(arg_keys[12], 71), 0),
    }


def local_filter(residues, log_rate, positions):
    rate = jnp.exp(log_rate)
    amplitude = residues * jnp.sqrt(2.0 * rate)

    def add_mode(total, pair):
        amp_col, rate_col = pair
        return (total + amp_col[:, None] * jnp.exp(-rate_col[:, None] * positions[None, :]), None)
    start = jnp.zeros((residues.shape[0], positions.shape[0]), jnp.float32)
    total, unused = lax.scan(add_mode, start, (amplitude.T, rate.T))
    return total

def filter_pullback(fgrad, residues, log_rate, positions):
    rate = jnp.exp(log_rate)
    root = jnp.sqrt(2.0 * rate)
    amplitude = residues * root

    def moments(rate_col):
        decay = jnp.exp(-rate_col[:, None] * positions[None, :])
        weighted = fgrad * decay
        return (lax.optimization_barrier(jnp.sum(weighted, axis=-1)), lax.optimization_barrier(jnp.sum(weighted * positions[None, :], axis=-1)))
    zero, one = lax.map(moments, rate.T)
    zero = zero.T
    one = one.T
    return (root * zero, amplitude * (0.5 * zero - rate * one))

def operator_grads(source, signal, residues, log_rate, positions):
    size = 2 * LENGTH
    filt = local_filter(residues, log_rate, positions)
    spec_filter = jnp.fft.rfft(filt, n=size, axis=-1)
    spec_source = jnp.fft.rfft(source, n=size, axis=-1)
    spec_signal = jnp.fft.rfft(signal, n=size, axis=-1)
    back = jnp.fft.irfft(jnp.conj(spec_filter)[None] * spec_source, n=size, axis=-1)[..., :LENGTH]
    fgrad = jnp.fft.irfft(lax.optimization_barrier(jnp.sum(spec_source * jnp.conj(spec_signal), axis=0)), n=size, axis=-1)[..., :LENGTH]
    grad_res, grad_log = filter_pullback(fgrad.astype(filt.dtype), residues, log_rate, positions)
    return (back.astype(filt.dtype), grad_res, grad_log)

def reference(value, key_one, gate_one, conv_one, key_two, gate_two, conv_two, grad_out, residues_one, log_rate_one, residues_two, log_rate_two):
    positions = jnp.arange(LENGTH).astype(jnp.float32)
    scale = 1.0 / math.sqrt(BATCH * LENGTH)
    through = gate_one.astype(jnp.float32) * conv_one.astype(jnp.float32)
    signal_two = key_two.astype(jnp.float32) * through
    signal_one = key_one.astype(jnp.float32) * value.astype(jnp.float32)
    grad_gate_two = (grad_out.astype(jnp.float32) * conv_two.astype(jnp.float32)).astype(jnp.bfloat16)
    source_two = grad_out.astype(jnp.float32) * gate_two.astype(jnp.float32)
    back_two, res_two, log_two = operator_grads(source_two, signal_two, residues_two, log_rate_two, positions)
    grad_key_two = (back_two * through).astype(jnp.bfloat16)
    grad_through = back_two * key_two.astype(jnp.float32)
    grad_gate_one = (grad_through * conv_one.astype(jnp.float32)).astype(jnp.bfloat16)
    source_one = grad_through * gate_one.astype(jnp.float32)
    back_one, res_one, log_one = operator_grads(source_one, signal_one, residues_one, log_rate_one, positions)
    grad_key_one = (back_one * value.astype(jnp.float32)).astype(jnp.bfloat16)
    grad_value = (back_one * key_one.astype(jnp.float32)).astype(jnp.bfloat16)
    return (grad_value, grad_key_one, grad_gate_one, grad_key_two, grad_gate_two, res_one * scale, log_one * scale, res_two * scale, log_two * scale)
```

```python
import math

import jax
import jax.numpy as jnp
from jax import lax
from jax.experimental import pallas as pl
from jax.experimental.pallas import tpu as pltpu
from jax.sharding import PartitionSpec as P

MESH = pl.DeviceIdType.MESH
LOCAL = 128
CHAN = 512
ORDER = 16
STATE = (8, 8, 128)
SCALE = 1.0 / math.sqrt(8192.0)
UNROLL = 4

(AMP1, RATE1, AMP2, RATE2, S2, M2, L02, L12, ZA1, ZB1, ZA2, ZB2, C2, S1, EU, EN, EN1, EN2) = range(18)


def wait_bytes(ref, sem):
    pltpu.make_async_copy(ref, ref, sem).wait()


def kernel(
    value, key_one, gate_one, conv_one, key_two, gate_two, grad_out, res1, lr1, res2, lr2,
    back1_out, back2_out, sums_out,
    wide, narrow, in_sem, src2_t, gain_t, sig1_t, sig2_t, src1_t, back2_t, back1_t, par,
    keep, usend, urecv, nsend, nrecv, vsend, vrecv, grads, rs_recv, zred, piece,
    us_sem, ur_sem, ns_sem, nr_sem, vs_sem, vr_sem, p_send, p_recv,
):
    dp = lax.axis_index("dp")
    ctx = lax.axis_index("context")
    y, x, z = ctx // 16, (ctx // 4) % 4, ctx % 4
    me = ctx // 4
    coords = (y, x, z)

    def at(axis, d):
        if axis == 0:
            return (dp, ((y + d) % 4) * 16 + x * 4 + z)
        if axis == 1:
            return (dp, y * 16 + ((x + d) % 4) * 4 + z)
        return (dp, y * 16 + x * 4 + (z + d) % 4)

    plane = [
        (((y + e) % 4) * 4 + (x + f) % 4) for e in range(4) for f in range(4) if e or f
    ]

    barrier = pltpu.get_barrier_semaphore()
    for q in plane:
        pl.semaphore_signal(barrier, inc=1, device_id=(dp, q * 4 + z), device_id_type=MESH)
    for d in (1, 2, 3):
        pl.semaphore_signal(barrier, inc=1, device_id=at(2, d), device_id_type=MESH)

    wide_in = (grad_out, gate_two, key_two, gate_one, conv_one, key_one, value)
    narrow_in = (lr2, lr1, res2, res1)
    loads = []
    for i, ref in enumerate(narrow_in):
        loads.append(pltpu.make_async_copy(ref, narrow.at[i], in_sem.at[7 + i]))
    for i, ref in enumerate(wide_in):
        loads.append(pltpu.make_async_copy(ref.at[0], wide.at[i], in_sem.at[i]))
    for load in loads:
        load.start()

    for i in range(4):
        loads[i].wait()
        for c in range(4):
            par[i, pl.ds(c, ORDER, stride=4), :] = narrow[i, c * 128 : (c + 1) * 128, :].T
    rate2 = jnp.exp(par[0]).reshape(STATE)
    rate1 = jnp.exp(par[1]).reshape(STATE)
    keep[RATE2] = rate2
    keep[RATE1] = rate1
    keep[AMP2] = par[2].reshape(STATE) * jnp.sqrt(2.0 * rate2)
    keep[AMP1] = par[3].reshape(STATE) * jnp.sqrt(2.0 * rate1)

    def block(i, c):
        return wide[i, c * 128 : (c + 1) * 128, :].astype(jnp.float32)

    def put(ref, c, tile):
        flipped = tile.T
        ref[pl.ds(c, LOCAL, stride=8), :] = flipped
        ref[pl.ds(c + 4, LOCAL, stride=8), :] = flipped

    def row(ref, t):
        return ref[pl.ds(pl.multiple_of(t * 8, 8), 8), :][None]

    zero = jnp.zeros(STATE, jnp.float32)

    loads[4].wait()
    loads[5].wait()
    for c in range(4):
        put(src2_t, c, block(0, c) * block(1, c))

    decay2 = jnp.exp(-rate2)

    def first(i, state):
        return decay2 * state + row(src2_t, LOCAL - 1 - i)

    state = lax.fori_loop(0, LOCAL, first, zero, unroll=UNROLL)
    keep[S2] = state
    usend[0, 0] = state

    for i in range(6, 11):
        loads[i].wait()
    for c in range(4):
        kt, go = block(2, c), block(3, c)
        put(gain_t, c, kt * go)
        put(sig2_t, c, kt * (go * block(4, c)))
        put(sig1_t, c, block(5, c) * block(6, c))

    decay1 = jnp.exp(-keep[RATE1])

    def ahead(t, st):
        a0, a1, b0, b1 = st
        u = a0 + row(sig1_t, t)
        v = b0 + row(sig2_t, t)
        return decay1 * u, decay1 * (a1 + u), decay2 * v, decay2 * (b1 + v)

    za1, zb1, za2, zb2 = lax.fori_loop(0, LOCAL, ahead, (zero,) * 4, unroll=UNROLL)
    keep[ZA1], keep[ZB1], keep[ZA2], keep[ZB2] = za1, zb1, za2, zb2
    nsend[0, 0, 0], nsend[0, 0, 1], nsend[0, 0, 2] = za1, zb1, za2

    pl.semaphore_wait(barrier, 18)

    def send(axis, buf, recv, ssem, rsem, suffix):
        for d in (1, 2, 3):
            which = 0 if axis == 0 else (coords[axis] + d) // 4
            pltpu.make_async_remote_copy(
                src_ref=buf.at[axis, which],
                dst_ref=recv.at[axis, 3 - d if suffix else d - 1],
                send_sem=ssem.at[axis],
                recv_sem=rsem.at[axis],
                device_id=at(axis, d),
                device_id_type=MESH,
            ).start()

    strides = (2048.0, 512.0, 128.0)

    def masked(axis, array, d, suffix):
        if axis:
            return array
        there = (y + d < 4) if suffix else (y >= d)
        return jnp.where(there, array, 0.0)

    def suffix_merge(axis, recv, rsem, far, rate):
        wait_bytes(recv.at[axis], rsem.at[axis])
        power = jnp.exp(-strides[axis] * rate)
        for d in (3, 2, 1):
            far = masked(axis, recv[axis, d - 1], d, True) + power * far
        return far, power

    def prefix_merge(axis):
        wait_bytes(nrecv.at[axis], nr_sem.at[axis])
        step = strides[axis]
        p1 = jnp.exp(-step * keep[RATE1])
        p2 = jnp.exp(-step * keep[RATE2])
        if axis == 0:
            f0, f1, f2 = zero, zero, zero
        else:
            f0, f1, f2 = keep[EN], keep[EN1], keep[EN2]
        for d in (3, 2, 1):
            f1 = masked(axis, nrecv[axis, d - 1, 1], d, False) + p1 * (f1 + step * f0)
            f0 = masked(axis, nrecv[axis, d - 1, 0], d, False) + p1 * f0
            f2 = masked(axis, nrecv[axis, d - 1, 2], d, False) + p2 * f2
        keep[EN], keep[EN1], keep[EN2] = f0, f1, f2
        if axis < 2:
            nsend[axis + 1, 1, 0], nsend[axis + 1, 1, 1], nsend[axis + 1, 1, 2] = f0, f1, f2
            nsend[axis + 1, 0, 0] = keep[ZA1] + p1 * f0
            nsend[axis + 1, 0, 1] = keep[ZB1] + p1 * (f1 + step * f0)
            nsend[axis + 1, 0, 2] = keep[ZA2] + p2 * f2

    def back_step(axis, buf, recv, ssem, rsem, own, rate):
        far = zero if axis == 0 else keep[EU]
        far, power = suffix_merge(axis, recv, rsem, far, keep[rate])
        keep[EU] = far
        if axis < 2:
            buf[axis + 1, 0] = far
            buf[axis + 1, 1] = keep[own] + power * far
            send(axis + 1, buf, recv, ssem, rsem, True)
        return far

    send(0, usend, urecv, us_sem, ur_sem, True)
    send(0, nsend, nrecv, ns_sem, nr_sem, False)

    def near(src_t, sig_t, decay):
        def body(i, st):
            t = LOCAL - 1 - i
            x0, x1, l0, l1 = st
            x1 = decay * (x1 + x0)
            x0 = decay * x0 + row(src_t, t)
            sig = row(sig_t, t)
            return x0, x1, l0 + sig * x0, l1 + sig * x1

        return lax.fori_loop(0, LOCAL, body, (zero,) * 4, unroll=UNROLL)

    unused, m2, l02, l12 = near(src2_t, sig2_t, decay2)
    keep[M2], keep[L02], keep[L12] = m2, l02, l12

    back_step(0, usend, urecv, us_sem, ur_sem, S2, RATE2)
    prefix_merge(0)
    send(1, nsend, nrecv, ns_sem, nr_sem, False)
    back_step(1, usend, urecv, us_sem, ur_sem, S2, RATE2)
    prefix_merge(1)
    send(2, nsend, nrecv, ns_sem, nr_sem, False)
    c2 = back_step(2, usend, urecv, us_sem, ur_sem, S2, RATE2)
    keep[C2] = c2

    decay1 = jnp.exp(-keep[RATE1])
    decay2 = jnp.exp(-keep[RATE2])
    amp2 = keep[AMP2]

    def middle(i, st):
        t = LOCAL - 1 - i
        xa, xb = st
        xa = decay2 * xa + row(src2_t, t)
        part = jnp.sum(amp2 * xa, axis=0)
        back = part + pltpu.roll(part, 4, 0)
        here = pl.ds(pl.multiple_of(t * 8, 8), 8)
        back2_t[here, :] = back
        source = back * gain_t[here, :]
        src1_t[here, :] = source
        return xa, decay1 * xb + source[None]

    unused, s1 = lax.fori_loop(0, LOCAL, middle, (c2, zero), unroll=UNROLL)
    keep[S1] = s1
    vsend[0, 0] = s1
    send(0, vsend, vrecv, vs_sem, vr_sem, True)

    unused, m1, l01, l11 = near(src1_t, sig1_t, decay1)
    prefix_merge(2)
    y1, y11, y2 = keep[EN], keep[EN1], keep[EN2]
    rate1, amp1 = keep[RATE1], keep[AMP1]
    zero_sum = l01 + s1 * y1
    one_sum = l11 + s1 * y11 + m1 * y1
    grads[0] = zero_sum * jnp.sqrt(2.0 * rate1) * SCALE
    grads[1] = amp1 * (0.5 * zero_sum - rate1 * one_sum) * SCALE
    rate2, amp2 = keep[RATE2], keep[AMP2]
    c2 = keep[C2]
    zero_sum = keep[L02] + keep[ZA2] * c2
    one_sum = keep[L12] + keep[ZB2] * c2 + keep[M2] * y2 + (128.0 * jnp.exp(-128.0 * rate2)) * (y2 * c2)
    grads[2] = zero_sum * jnp.sqrt(2.0 * rate2) * SCALE
    grads[3] = amp2 * (0.5 * zero_sum - rate2 * one_sum) * SCALE

    def share(ref, q):
        return ref.at[q // 4, pl.ds((q % 4) * 2, 2)]

    for i, q in enumerate(plane):
        pltpu.make_async_remote_copy(
            src_ref=share(grads, q), dst_ref=rs_recv.at[i], send_sem=p_send.at[0], recv_sem=p_recv.at[0],
            device_id=(dp, q * 4 + z), device_id_type=MESH,
        ).start()

    back_step(0, vsend, vrecv, vs_sem, vr_sem, S1, RATE1)

    wait_bytes(rs_recv, p_recv.at[0])
    total = grads[me // 4, pl.ds((me % 4) * 2, 2)]
    for i in range(15):
        total = total + rs_recv[i]
    zred[z] = total
    for d in (1, 2, 3):
        pltpu.make_async_remote_copy(
            src_ref=zred.at[z], dst_ref=zred.at[z], send_sem=p_send.at[1], recv_sem=p_recv.at[1],
            device_id=at(2, d), device_id_type=MESH,
        ).start()

    back_step(1, vsend, vrecv, vs_sem, vr_sem, S1, RATE1)

    for c in range(4):
        back2_out[c * 128 : (c + 1) * 128, :] = back2_t[pl.ds(c, LOCAL, stride=8), :].T

    wait_bytes(zred.at[pl.ds(0, 3)], p_recv.at[1])
    total = (zred[0] + zred[1]) + (zred[2] + zred[3])
    piece[...] = total
    sums_out[me] = total
    for i, q in enumerate(plane):
        pltpu.make_async_remote_copy(
            src_ref=piece, dst_ref=sums_out.at[me], send_sem=p_send.at[2], recv_sem=p_recv.at[2],
            device_id=(dp, q * 4 + z), device_id_type=MESH,
        ).start()

    c1 = back_step(2, vsend, vrecv, vs_sem, vr_sem, S1, RATE1)
    decay1 = jnp.exp(-keep[RATE1])
    amp1 = keep[AMP1]

    def last(i, xa):
        t = LOCAL - 1 - i
        xa = decay1 * xa + row(src1_t, t)
        part = jnp.sum(amp1 * xa, axis=0)
        back1_t[pl.ds(pl.multiple_of(t * 8, 8), 8), :] = part + pltpu.roll(part, 4, 0)
        return xa

    lax.fori_loop(0, LOCAL, last, c1, unroll=UNROLL)
    for c in range(4):
        back1_out[c * 128 : (c + 1) * 128, :] = back1_t[pl.ds(c, LOCAL, stride=8), :].T

    for axis in range(3):
        wait_bytes(urecv.at[axis], us_sem.at[axis])
        wait_bytes(nrecv.at[axis], ns_sem.at[axis])
        wait_bytes(vrecv.at[axis], vs_sem.at[axis])
    wait_bytes(rs_recv, p_send.at[0])
    wait_bytes(zred.at[pl.ds(0, 3)], p_send.at[1])
    wait_bytes(rs_recv, p_send.at[2])
    wait_bytes(sums_out.at[pl.ds(0, 15)], p_recv.at[2])


def per_device(
    value, key_one, gate_one, conv_one, key_two, gate_two, conv_two, grad_out,
    residues_one, log_rate_one, residues_two, log_rate_two,
):
    f32 = jnp.float32
    vmem = pltpu.VMEM
    dma = pltpu.SemaphoreType.DMA
    turned = vmem((LOCAL * 8, 128), f32)
    back_one, back_two, sums = pl.pallas_call(
        kernel,
        out_shape=[
            jax.ShapeDtypeStruct((CHAN, LOCAL), f32),
            jax.ShapeDtypeStruct((CHAN, LOCAL), f32),
            jax.ShapeDtypeStruct((16, 2, 8, 128), f32),
        ],
        in_specs=[pl.BlockSpec(memory_space=pl.ANY)] * 11,
        out_specs=[pl.BlockSpec(memory_space=pltpu.VMEM)] * 3,
        scratch_shapes=[
            vmem((7, CHAN, LOCAL), jnp.bfloat16),
            vmem((4, CHAN, ORDER), f32),
            dma((11,)),
            turned, turned, turned, turned, turned, turned, turned,
            vmem((4, 64, 128), f32),
            vmem((18,) + STATE, f32),
            vmem((3, 2) + STATE, f32),
            vmem((3, 3) + STATE, f32),
            vmem((3, 2, 3) + STATE, f32),
            vmem((3, 3, 3) + STATE, f32),
            vmem((3, 2) + STATE, f32),
            vmem((3, 3) + STATE, f32),
            vmem((4,) + STATE, f32),
            vmem((15, 2, 8, 128), f32),
            vmem((4, 2, 8, 128), f32),
            vmem((2, 8, 128), f32),
            dma((3,)), dma((3,)), dma((3,)), dma((3,)), dma((3,)), dma((3,)), dma((3,)), dma((3,)),
        ],
        compiler_params=pltpu.CompilerParams(
            collective_id=0, has_side_effects=True, vmem_limit_bytes=32 * 1024 * 1024
        ),
        name="hyena_back",
    )(
        value, key_one, gate_one, conv_one, key_two, gate_two, grad_out,
        residues_one, log_rate_one, residues_two, log_rate_two,
    )

    def widen(array):
        return array.astype(f32)

    def rounded(array):
        return array.astype(jnp.bfloat16)

    back_one, back_two = back_one[None], back_two[None]
    grad_gate_two = rounded(widen(grad_out) * widen(conv_two))
    grad_key_two = rounded(back_two * (widen(gate_one) * widen(conv_one)))
    grad_gate_one = rounded(back_two * widen(key_two) * widen(conv_one))
    grad_key_one = rounded(back_one * widen(value))
    grad_value = rounded(back_one * widen(key_one))
    grads = sums.reshape(4, ORDER, 4, 128).transpose(0, 2, 3, 1).reshape(4, CHAN, ORDER)
    return (
        grad_value, grad_key_one, grad_gate_one, grad_key_two, grad_gate_two,
        grads[0], grads[1], grads[2], grads[3],
    )


def solution(mesh):
    wide = P(None, "dp", "context")
    thin = P("dp", None)
    return jax.shard_map(
        per_device,
        mesh=mesh,
        in_specs=(wide,) * 8 + (thin,) * 4,
        out_specs=(wide,) * 5 + (thin,) * 4,
        check_vma=False,
    )
```

```python
import math

import jax
import jax.numpy as jnp
from jax import lax
from jax.experimental import pallas as pl
from jax.experimental.pallas import tpu as pltpu
from jax.sharding import PartitionSpec as P

MESH = pl.DeviceIdType.MESH
LOCAL = 128
CHAN = 512
ORDER = 16
STATE = (8, 8, 128)
SCALE = 1.0 / math.sqrt(8192.0)
UNROLL = 4

(AMP1, RATE1, AMP2, RATE2, S2, M2, L02, L12, ZA2, ZB2, C2, S1, EU) = range(13)


def wait_bytes(ref, sem):
    pltpu.make_async_copy(ref, ref, sem).wait()


def kernel(
    value, key_one, gate_one, conv_one, key_two, gate_two, conv_two, grad_out, res1, lr1, res2, lr2,
    value_out, key1_out, gate1_out, key2_out, gate2_out, sums_out,
    wide, narrow, made, sums, in_sem, src2_t, gain_t, sig1_t, sig2_t, src1_t, back2_t, back1_t, par,
    keep, usend, urecv, nsend, nrecv, tsend, trecv, ysend, yrecv, vsend, vrecv, grads, rs_recv, zred, piece,
    us_sem, ur_sem, n_sem, ts_sem, tr_sem, vs_sem, vr_sem, p_send, p_recv, out_sem,
):
    dp = lax.axis_index("dp")
    ctx = lax.axis_index("context")
    y, x, z = ctx // 16, (ctx // 4) % 4, ctx % 4
    me = ctx // 4
    coords = (y, x, z)

    def at(axis, d):
        if axis == 0:
            return (dp, ((y + d) % 4) * 16 + x * 4 + z)
        if axis == 1:
            return (dp, y * 16 + ((x + d) % 4) * 4 + z)
        return (dp, y * 16 + x * 4 + (z + d) % 4)

    plane = [
        (((y + e) % 4) * 4 + (x + f) % 4) for e in range(4) for f in range(4) if e or f
    ]

    barrier = pltpu.get_barrier_semaphore()
    for q in plane:
        pl.semaphore_signal(barrier, inc=1, device_id=(dp, q * 4 + z), device_id_type=MESH)
    for d in (1, 2, 3):
        pl.semaphore_signal(barrier, inc=1, device_id=at(2, d), device_id_type=MESH)

    wide_in = (grad_out, gate_two, key_two, gate_one, conv_one, key_one, value, conv_two)
    narrow_in = (lr2, lr1, res2, res1)
    loads = []
    for i, ref in enumerate(narrow_in):
        loads.append(pltpu.make_async_copy(ref, narrow.at[i], in_sem.at[8 + i]))
    for i, ref in enumerate(wide_in):
        loads.append(pltpu.make_async_copy(ref.at[0], wide.at[i], in_sem.at[i]))
    for load in loads:
        load.start()

    for i in range(4):
        loads[i].wait()
        for c in range(4):
            par[i, pl.ds(c, ORDER, stride=4), :] = narrow[i, :, c * 128 : (c + 1) * 128]
    rate2 = jnp.exp(par[0]).reshape(STATE)
    rate1 = jnp.exp(par[1]).reshape(STATE)
    keep[RATE2] = rate2
    keep[RATE1] = rate1
    keep[AMP2] = par[2].reshape(STATE) * jnp.sqrt(2.0 * rate2)
    keep[AMP1] = par[3].reshape(STATE) * jnp.sqrt(2.0 * rate1)

    def block(i, c):
        return wide[i, c * 128 : (c + 1) * 128, :].astype(jnp.float32)

    def put(ref, c, tile):
        flipped = tile.T
        ref[pl.ds(c, LOCAL, stride=8), :] = flipped
        ref[pl.ds(c + 4, LOCAL, stride=8), :] = flipped

    def row(ref, t):
        return ref[pl.ds(pl.multiple_of(t * 8, 8), 8), :][None]

    zero = jnp.zeros(STATE, jnp.float32)

    loads[4].wait()
    loads[5].wait()
    for c in range(4):
        put(src2_t, c, block(0, c) * block(1, c))

    decay2 = jnp.exp(-rate2)

    def first(i, state):
        return decay2 * state + row(src2_t, LOCAL - 1 - i)

    state = lax.fori_loop(0, LOCAL, first, zero, unroll=UNROLL)
    keep[S2] = state
    usend[0, 0] = state

    for i in range(6, 12):
        loads[i].wait()
    for c in range(4):
        kt, go = block(2, c), block(3, c)
        put(gain_t, c, kt * go)
        put(sig2_t, c, kt * (go * block(4, c)))
        put(sig1_t, c, block(5, c) * block(6, c))

    decay1 = jnp.exp(-keep[RATE1])

    def ahead(t, st):
        a0, a1, b0, b1 = st
        u = a0 + row(sig1_t, t)
        v = b0 + row(sig2_t, t)
        return decay1 * u, decay1 * (a1 + u), decay2 * v, decay2 * (b1 + v)

    za1, zb1, za2, zb2 = lax.fori_loop(0, LOCAL, ahead, (zero,) * 4, unroll=UNROLL)
    keep[ZA2], keep[ZB2] = za2, zb2
    for k, array in enumerate((za1, zb1, za2)):
        nsend[:, k] = array.reshape(4, 2, 8, 128)

    pl.semaphore_wait(barrier, 18)

    def send(axis, buf, recv, ssem, rsem):
        for d in (1, 2, 3):
            which = 0 if axis == 0 else (coords[axis] + d) // 4
            pltpu.make_async_remote_copy(
                src_ref=buf.at[axis, which],
                dst_ref=recv.at[axis, 3 - d],
                send_sem=ssem.at[axis],
                recv_sem=rsem.at[axis],
                device_id=at(axis, d),
                device_id_type=MESH,
            ).start()

    strides = (2048.0, 512.0, 128.0)

    def masked(axis, array, d):
        return array if axis else jnp.where(y + d < 4, array, 0.0)

    def suffix_merge(axis, recv, rsem, far, rate):
        wait_bytes(recv.at[axis], rsem.at[axis])
        power = jnp.exp(-strides[axis] * rate)
        for d in (3, 2, 1):
            far = masked(axis, recv[axis, d - 1], d) + power * far
        return far, power

    def spread_signals():
        for d in (1, 2, 3):
            pltpu.make_async_remote_copy(
                src_ref=nsend.at[(z + d) % 4], dst_ref=nrecv.at[z], send_sem=n_sem.at[0], recv_sem=n_sem.at[1],
                device_id=at(2, d), device_id_type=MESH,
            ).start()
        nrecv[z] = nsend[z]

    def quarter_rates():
        return keep[RATE1, pl.ds(2 * z, 2)], keep[RATE2, pl.ds(2 * z, 2)]

    def shifted(state, length, powers):
        f0, f1, f2 = state
        return powers[0] * f0, powers[0] * (f1 + length * f0), powers[1] * f2

    def added(left, right):
        return tuple(p + q for p, q in zip(left, right))

    def line(i):
        return tuple(nrecv[i, k] for k in range(3))

    def total_lines():
        wait_bytes(nrecv.at[pl.ds(0, 3)], n_sem.at[1])
        powers = tuple(jnp.exp(-128.0 * rate) for rate in quarter_rates())
        state = line(0)
        for i in (1, 2, 3):
            state = added(line(i), shifted(state, 128.0, powers))
        for k in range(3):
            tsend[k] = state[k]
        for k in range(1, 16):
            @pl.when(me + k < 16)
            def _():
                pltpu.make_async_remote_copy(
                    src_ref=tsend, dst_ref=trecv.at[k - 1], send_sem=ts_sem.at[k - 1], recv_sem=tr_sem.at[k - 1],
                    device_id=(dp, (me + k) * 4 + z), device_id_type=MESH,
                ).start()


    def return_signals():
        near_powers = []
        powers = []
        for rate in quarter_rates():
            powers.append(jnp.exp(-512.0 * rate))
            near_powers.append(jnp.exp(-128.0 * rate))
        for k in range(1, 16):
            @pl.when(me >= k)
            def _():
                wait_bytes(trecv.at[k - 1], tr_sem.at[k - 1])
        state = tuple(jnp.zeros((2, 8, 128), jnp.float32) for _ in range(3))
        for k in range(15, 0, -1):
            there = me >= k
            block = tuple(jnp.where(there, trecv[k - 1, i], 0.0) for i in range(3))
            state = added(block, shifted(state, 512.0, powers))
        for i in range(4):
            for k in range(3):
                ysend[i, k] = state[k]
            state = added(line(i), shifted(state, 128.0, near_powers))
        for d in (1, 2, 3):
            pltpu.make_async_remote_copy(
                src_ref=ysend.at[(z + d) % 4], dst_ref=yrecv.at[z], send_sem=n_sem.at[2], recv_sem=n_sem.at[3],
                device_id=at(2, d), device_id_type=MESH,
            ).start()
        yrecv[z] = ysend[z]

    def back_step(axis, buf, recv, ssem, rsem, own, rate):
        far = zero if axis == 0 else keep[EU]
        far, power = suffix_merge(axis, recv, rsem, far, keep[rate])
        keep[EU] = far
        if axis < 2:
            buf[axis + 1, 0] = far
            buf[axis + 1, 1] = keep[own] + power * far
            send(axis + 1, buf, recv, ssem, rsem)
        return far

    send(0, usend, urecv, us_sem, ur_sem)
    spread_signals()

    def near(src_t, sig_t, decay):
        def body(i, st):
            t = LOCAL - 1 - i
            x0, x1, l0, l1 = st
            x1 = decay * (x1 + x0)
            x0 = decay * x0 + row(src_t, t)
            sig = row(sig_t, t)
            return x0, x1, l0 + sig * x0, l1 + sig * x1

        return lax.fori_loop(0, LOCAL, body, (zero,) * 4, unroll=UNROLL)

    unused, m2, l02, l12 = near(src2_t, sig2_t, decay2)
    keep[M2], keep[L02], keep[L12] = m2, l02, l12

    back_step(0, usend, urecv, us_sem, ur_sem, S2, RATE2)
    back_step(1, usend, urecv, us_sem, ur_sem, S2, RATE2)
    total_lines()
    return_signals()
    c2 = back_step(2, usend, urecv, us_sem, ur_sem, S2, RATE2)
    keep[C2] = c2

    decay1 = jnp.exp(-keep[RATE1])
    decay2 = jnp.exp(-keep[RATE2])
    amp2 = keep[AMP2]

    def middle(i, st):
        t = LOCAL - 1 - i
        xa, xb = st
        xa = decay2 * xa + row(src2_t, t)
        part = jnp.sum(amp2 * xa, axis=0)
        back = part + pltpu.roll(part, 4, 0)
        here = pl.ds(pl.multiple_of(t * 8, 8), 8)
        back2_t[here, :] = back
        source = back * gain_t[here, :]
        src1_t[here, :] = source
        return xa, decay1 * xb + source[None]

    unused, s1 = lax.fori_loop(0, LOCAL, middle, (c2, zero), unroll=UNROLL)
    keep[S1] = s1
    vsend[0, 0] = s1
    send(0, vsend, vrecv, vs_sem, vr_sem)

    unused, m1, l01, l11 = near(src1_t, sig1_t, decay1)
    wait_bytes(yrecv.at[pl.ds(0, 3)], n_sem.at[3])
    y1, y11, y2 = (yrecv[:, k].reshape(STATE) for k in range(3))
    rate1, amp1 = keep[RATE1], keep[AMP1]
    zero_sum = l01 + s1 * y1
    one_sum = l11 + s1 * y11 + m1 * y1
    grads[0] = zero_sum * jnp.sqrt(2.0 * rate1) * SCALE
    grads[1] = amp1 * (0.5 * zero_sum - rate1 * one_sum) * SCALE
    rate2, amp2 = keep[RATE2], keep[AMP2]
    c2 = keep[C2]
    zero_sum = keep[L02] + keep[ZA2] * c2
    one_sum = keep[L12] + keep[ZB2] * c2 + keep[M2] * y2 + (128.0 * jnp.exp(-128.0 * rate2)) * (y2 * c2)
    grads[2] = zero_sum * jnp.sqrt(2.0 * rate2) * SCALE
    grads[3] = amp2 * (0.5 * zero_sum - rate2 * one_sum) * SCALE

    def share(ref, q):
        return ref.at[q // 4, pl.ds((q % 4) * 2, 2)]

    for i, q in enumerate(plane):
        pltpu.make_async_remote_copy(
            src_ref=share(grads, q), dst_ref=rs_recv.at[i], send_sem=p_send.at[0], recv_sem=p_recv.at[0],
            device_id=(dp, q * 4 + z), device_id_type=MESH,
        ).start()

    back_step(0, vsend, vrecv, vs_sem, vr_sem, S1, RATE1)

    wait_bytes(rs_recv, p_recv.at[0])
    total = grads[me // 4, pl.ds((me % 4) * 2, 2)]
    for i in range(15):
        total = total + rs_recv[i]
    zred[z] = total
    for d in (1, 2, 3):
        pltpu.make_async_remote_copy(
            src_ref=zred.at[z], dst_ref=zred.at[z], send_sem=p_send.at[1], recv_sem=p_recv.at[1],
            device_id=at(2, d), device_id_type=MESH,
        ).start()

    back_step(1, vsend, vrecv, vs_sem, vr_sem, S1, RATE1)

    outs = (value_out, key1_out, gate1_out, key2_out, gate2_out)

    def emit(i):
        pltpu.make_async_copy(made.at[i], outs[i].at[0], out_sem.at[i]).start()

    def store(i, c, tile):
        made[i, c * 128 : (c + 1) * 128, :] = tile.astype(jnp.bfloat16)

    for c in range(4):
        back = back2_t[pl.ds(c, LOCAL, stride=8), :].T
        store(2, c, back * block(2, c) * block(4, c))
        store(3, c, back * (block(3, c) * block(4, c)))
        store(4, c, block(0, c) * block(7, c))
    for i in (2, 3, 4):
        emit(i)

    wait_bytes(zred.at[pl.ds(0, 3)], p_recv.at[1])
    total = (zred[0] + zred[1]) + (zred[2] + zred[3])
    piece[...] = total
    sums[me] = total
    for i, q in enumerate(plane):
        pltpu.make_async_remote_copy(
            src_ref=piece, dst_ref=sums.at[me], send_sem=p_send.at[2], recv_sem=p_recv.at[2],
            device_id=(dp, q * 4 + z), device_id_type=MESH,
        ).start()

    c1 = back_step(2, vsend, vrecv, vs_sem, vr_sem, S1, RATE1)
    decay1 = jnp.exp(-keep[RATE1])
    amp1 = keep[AMP1]

    def last(i, xa):
        t = LOCAL - 1 - i
        xa = decay1 * xa + row(src1_t, t)
        part = jnp.sum(amp1 * xa, axis=0)
        back1_t[pl.ds(pl.multiple_of(t * 8, 8), 8), :] = part + pltpu.roll(part, 4, 0)
        return xa

    lax.fori_loop(0, LOCAL, last, c1, unroll=UNROLL)
    for c in range(4):
        back = back1_t[pl.ds(c, LOCAL, stride=8), :].T
        store(0, c, back * block(5, c))
        store(1, c, back * block(6, c))
    for i in (0, 1):
        emit(i)

    wait_bytes(sums.at[pl.ds(0, 15)], p_recv.at[2])
    last_copy = pltpu.make_async_copy(sums, sums_out, out_sem.at[5])
    last_copy.start()
    for axis in range(3):
        wait_bytes(urecv.at[axis], us_sem.at[axis])
        wait_bytes(vrecv.at[axis], vs_sem.at[axis])
    wait_bytes(nrecv.at[pl.ds(0, 3)], n_sem.at[0])
    wait_bytes(yrecv.at[pl.ds(0, 3)], n_sem.at[2])
    for k in range(1, 16):
        @pl.when(me + k < 16)
        def _():
            wait_bytes(tsend, ts_sem.at[k - 1])
    wait_bytes(rs_recv, p_send.at[0])
    wait_bytes(zred.at[pl.ds(0, 3)], p_send.at[1])
    wait_bytes(rs_recv, p_send.at[2])
    for i in range(5):
        pltpu.make_async_copy(made.at[i], outs[i].at[0], out_sem.at[i]).wait()
    last_copy.wait()


def hand_over(*refs):
    made, sums, outs, held, turned, thin, sem_in, sem_out = refs[:5], refs[5], refs[6:15], *refs[15:]
    loads = [pltpu.make_async_copy(made[i], held.at[i], sem_in.at[i]) for i in range(5)]
    loads.append(pltpu.make_async_copy(sums, turned, sem_in.at[5]))
    stores = [pltpu.make_async_copy(held.at[i], outs[i], sem_out.at[i]) for i in range(5)]
    stores += [pltpu.make_async_copy(thin.at[i], outs[5 + i], sem_out.at[5 + i]) for i in range(4)]
    for load in loads:
        load.start()
    for i in range(5):
        loads[i].wait()
        stores[i].start()
    loads[5].wait()
    for i in range(4):
        for c in range(4):
            thin[i, :, c * 128 : (c + 1) * 128] = turned[pl.ds(i * 64 + c, ORDER, stride=4), :]
        stores[5 + i].start()
    for store in stores:
        store.wait()


def per_device(
    value, key_one, gate_one, conv_one, key_two, gate_two, conv_two, grad_out,
    residues_one, log_rate_one, residues_two, log_rate_two,
):
    f32 = jnp.float32
    vmem = pltpu.VMEM
    dma = pltpu.SemaphoreType.DMA
    turned = vmem((LOCAL * 8, 128), f32)
    bf16 = jnp.bfloat16
    shape = value.shape
    anywhere = pl.BlockSpec(memory_space=pl.ANY)
    made = pl.pallas_call(
        kernel,
        out_shape=[jax.ShapeDtypeStruct(shape, bf16)] * 5 + [jax.ShapeDtypeStruct((16, 2, 8, 128), f32)],
        in_specs=[anywhere] * 12,
        out_specs=[anywhere] * 6,
        scratch_shapes=[
            vmem((8, CHAN, LOCAL), bf16),
            vmem((4, ORDER, CHAN), f32),
            vmem((5, CHAN, LOCAL), bf16),
            vmem((16, 2, 8, 128), f32),
            dma((12,)),
            turned, turned, turned, turned, turned, turned, turned,
            vmem((4, 64, 128), f32),
            vmem((13,) + STATE, f32),
            vmem((3, 2) + STATE, f32),
            vmem((3, 3) + STATE, f32),
            vmem((4, 3, 2, 8, 128), f32),
            vmem((4, 3, 2, 8, 128), f32),
            vmem((3, 2, 8, 128), f32),
            vmem((15, 3, 2, 8, 128), f32),
            vmem((4, 3, 2, 8, 128), f32),
            vmem((4, 3, 2, 8, 128), f32),
            vmem((3, 2) + STATE, f32),
            vmem((3, 3) + STATE, f32),
            vmem((4,) + STATE, f32),
            vmem((15, 2, 8, 128), f32),
            vmem((4, 2, 8, 128), f32),
            vmem((2, 8, 128), f32),
            dma((3,)), dma((3,)), dma((4,)), dma((15,)), dma((15,)), dma((3,)), dma((3,)), dma((3,)), dma((3,)), dma((6,)),
        ],
        compiler_params=pltpu.CompilerParams(
            collective_id=0, has_side_effects=True, vmem_limit_bytes=56 * 1024 * 1024
        ),
        name="hyena_back",
    )(
        value, key_one, gate_one, conv_one, key_two, gate_two, conv_two, grad_out,
        residues_one.T, log_rate_one.T, residues_two.T, log_rate_two.T,
    )
    made = list(made[:5]) + [made[5].reshape(4 * ORDER * 4, 128)]
    thin = jax.ShapeDtypeStruct((ORDER, CHAN), f32)
    outs = pl.pallas_call(
        hand_over,
        out_shape=[jax.ShapeDtypeStruct(shape, bf16)] * 5 + [thin] * 4,
        in_specs=[anywhere] * 6,
        out_specs=[anywhere] * 9,
        scratch_shapes=[
            vmem((5,) + shape, bf16),
            vmem((4 * ORDER * 4, 128), f32),
            vmem((4, ORDER, CHAN), f32),
            dma((6,)),
            dma((9,)),
        ],
        name="hand_over",
    )(*made)
    return tuple(outs[:5]) + tuple(out.T for out in outs[5:])


def solution(mesh):
    wide = P(None, "dp", "context")
    thin = P("dp", None)
    return jax.shard_map(
        per_device,
        mesh=mesh,
        in_specs=(wide,) * 8 + (thin,) * 4,
        out_specs=(wide,) * 5 + (thin,) * 4,
        check_vma=False,
    )
```

```python
import math

import jax
import jax.numpy as jnp
from jax import lax
from jax.experimental import pallas as pl
from jax.experimental.pallas import tpu as pltpu
from jax.sharding import PartitionSpec as P

MESH = pl.DeviceIdType.MESH
LOCAL = 128
CHAN = 512
ORDER = 16
STATE = (8, 8, 128)
SCALE = 1.0 / math.sqrt(8192.0)
UNROLL = 8
CUTS = 2

(AMP1, RATE1, AMP2, RATE2, S2, M2, L02, L12, ZA2, ZB2, C2, S1, EU, POW1, POW2) = (*range(13), 13, 16)


def wait_bytes(ref, sem):
    pltpu.make_async_copy(ref, ref, sem).wait()


def kernel(
    value, key_one, gate_one, conv_one, key_two, gate_two, conv_two, grad_out, res1, lr1, res2, lr2,
    value_out, key1_out, gate1_out, key2_out, gate2_out, sums_out,
    wide, narrow, made, in_sem, src2_t, gain_t, sig1_t, sig2_t, src1_t, back2_t, back1_t, par,
    keep, usend, urecv, nsend, nrecv, tsend, trecv, ysend, yrecv, vsend, vrecv, grads, rs_recv, zred, piece,
    us_sem, ur_sem, n_sem, ts_sem, tr_sem, vs_sem, vr_sem, p_send, p_recv, out_sem,
):
    dp = lax.axis_index("dp")
    ctx = lax.axis_index("context")
    y, x, z = ctx // 16, (ctx // 4) % 4, ctx % 4
    me = ctx // 4
    coords = (y, x, z)

    def at(axis, d):
        if axis == 0:
            return (dp, ((y + d) % 4) * 16 + x * 4 + z)
        if axis == 1:
            return (dp, y * 16 + ((x + d) % 4) * 4 + z)
        return (dp, y * 16 + x * 4 + (z + d) % 4)

    plane = [
        (((y + e) % 4) * 4 + (x + f) % 4) for e in (2, 1, 3, 0) for f in (2, 1, 3, 0) if e or f
    ]

    barrier = pltpu.get_barrier_semaphore()
    for d in (2, 1, 3):
        pl.semaphore_signal(barrier, inc=1, device_id=at(2, d), device_id_type=MESH)

    trecv[...] = jnp.zeros(trecv.shape, jnp.float32)
    urecv[0] = jnp.zeros(urecv.shape[1:], jnp.float32)
    vrecv[0] = jnp.zeros(vrecv.shape[1:], jnp.float32)

    for axis in (0, 1):
        for d in (2, 1, 3):
            pl.semaphore_signal(barrier, inc=1, device_id=at(axis, d), device_id_type=MESH)

    wide_in = (grad_out, gate_two, key_two, gate_one, conv_one, key_one, value, conv_two)
    narrow_in = (lr2, lr1, res2, res1)
    loads = []
    for i, ref in enumerate(narrow_in):
        loads.append(pltpu.make_async_copy(ref, narrow.at[i], in_sem.at[8 + i]))
    for i, ref in enumerate(wide_in):
        loads.append(pltpu.make_async_copy(ref.at[0], wide.at[i], in_sem.at[i]))
    for load in loads:
        load.start()

    for i in range(4):
        loads[i].wait()
        for c in range(4):
            par[i, pl.ds(c, ORDER, stride=4), :] = narrow[i, :, c * 128 : (c + 1) * 128]
    rate2 = jnp.exp(par[0]).reshape(STATE)
    rate1 = jnp.exp(par[1]).reshape(STATE)
    keep[RATE2] = rate2
    keep[RATE1] = rate1
    keep[AMP2] = par[2].reshape(STATE) * jnp.sqrt(2.0 * rate2)
    keep[AMP1] = par[3].reshape(STATE) * jnp.sqrt(2.0 * rate1)

    def block(i, c):
        return wide[i, c * 128 : (c + 1) * 128, :].astype(jnp.float32)

    def put(ref, c, tile):
        flipped = tile.T
        ref[pl.ds(c, LOCAL, stride=8), :] = flipped
        ref[pl.ds(c + 4, LOCAL, stride=8), :] = flipped

    def row(ref, t):
        return ref[pl.ds(pl.multiple_of(t * 8, 8), 8), :][None]

    zero = jnp.zeros(STATE, jnp.float32)

    loads[4].wait()
    loads[5].wait()
    for c in range(4):
        put(src2_t, c, block(0, c) * block(1, c))

    decay2 = jnp.exp(-rate2)

    def first(i, state):
        return decay2 * state + row(src2_t, LOCAL - 1 - i)

    state = lax.fori_loop(0, LOCAL, first, zero, unroll=UNROLL)
    keep[S2] = state
    usend[0, 0] = state

    for i in range(6, 12):
        loads[i].wait()
    for c in range(4):
        kt, go = block(2, c), block(3, c)
        put(gain_t, c, kt * go)
        put(sig2_t, c, kt * (go * block(4, c)))
        put(sig1_t, c, block(5, c) * block(6, c))

    decay1 = jnp.exp(-keep[RATE1])

    def ahead(t, st):
        a0, a1, b0, b1 = st
        u = a0 + row(sig1_t, t)
        v = b0 + row(sig2_t, t)
        return decay1 * u, decay1 * (a1 + u), decay2 * v, decay2 * (b1 + v)

    za1, zb1, za2, zb2 = lax.fori_loop(0, LOCAL, ahead, (zero,) * 4, unroll=UNROLL)
    keep[ZA2], keep[ZB2] = za2, zb2
    for k, array in enumerate((za1, zb1, za2)):
        nsend[:, k] = array.reshape(4, 2, 8, 128)

    pl.semaphore_wait(barrier, 9)

    def send(axis, buf, recv, ssem, rsem):
        for d in (2, 1, 3):
            copy = pltpu.make_async_remote_copy(
                src_ref=buf.at[axis, 0 if axis == 0 else (coords[axis] + d) // 4],
                dst_ref=recv.at[axis, 3 - d],
                send_sem=ssem.at[d - 1 if axis == 0 else axis + 2],
                recv_sem=rsem.at[3 - d if axis == 0 else axis + 2],
                device_id=at(axis, d),
                device_id_type=MESH,
            )
            if axis:
                copy.start()
            else:
                pl.when(y + d >= 4)(copy.start)

    def arrived(axis, recv, rsem):
        if axis:
            wait_bytes(recv.at[axis], rsem.at[axis + 2])
        else:
            for d in (1, 2, 3):
                @pl.when(y + d < 4)
                def _():
                    wait_bytes(recv.at[0, d - 1], rsem.at[d - 1])

    def departed(axis, recv, ssem):
        if axis:
            wait_bytes(recv.at[axis], ssem.at[axis + 2])
        else:
            for d in (1, 2, 3):
                @pl.when(y + d >= 4)
                def _():
                    wait_bytes(recv.at[0, d - 1], ssem.at[d - 1])

    strides = (2048.0, 512.0, 128.0)

    def suffix_merge(axis, recv, rsem, far, rate):
        arrived(axis, recv, rsem)
        power = keep[rate + axis]
        for d in (3, 2, 1):
            far = recv[axis, d - 1] + power * far
        return far, power

    def spread_signals():
        for d in (2, 1, 3):
            pltpu.make_async_remote_copy(
                src_ref=nsend.at[(z + d) % 4], dst_ref=nrecv.at[z], send_sem=n_sem.at[0], recv_sem=n_sem.at[1],
                device_id=at(2, d), device_id_type=MESH,
            ).start()
        nrecv[z] = nsend[z]

    def quarter_rates():
        return keep[RATE1, pl.ds(2 * z, 2)], keep[RATE2, pl.ds(2 * z, 2)]

    def shifted(state, length, powers):
        f0, f1, f2 = state
        return powers[0] * f0, powers[0] * (f1 + length * f0), powers[1] * f2

    def added(left, right):
        return tuple(p + q for p, q in zip(left, right))

    def line(i):
        return tuple(nrecv[i, k] for k in range(3))

    def total_lines():
        wait_bytes(nrecv.at[pl.ds(0, 3)], n_sem.at[1])
        powers = tuple(jnp.exp(-128.0 * rate) for rate in quarter_rates())
        state = line(0)
        for i in (1, 2, 3):
            state = added(line(i), shifted(state, 128.0, powers))
        for k in range(3):
            tsend[k] = state[k]
        for k in range(15, 0, -1):
            @pl.when(me + k < 16)
            def _():
                pltpu.make_async_remote_copy(
                    src_ref=tsend, dst_ref=trecv.at[k - 1], send_sem=ts_sem.at[k - 1], recv_sem=tr_sem.at[k - 1],
                    device_id=(dp, (me + k) * 4 + z), device_id_type=MESH,
                ).start()


    def return_signals():
        near_powers = []
        powers = []
        for rate in quarter_rates():
            powers.append(jnp.exp(-512.0 * rate))
            near_powers.append(jnp.exp(-128.0 * rate))
        for k in range(1, 16):
            @pl.when(me >= k)
            def _():
                wait_bytes(trecv.at[k - 1], tr_sem.at[k - 1])
        state = tuple(jnp.zeros((2, 8, 128), jnp.float32) for _ in range(3))
        for k in range(15, 0, -1):
            block = tuple(trecv[k - 1, i] for i in range(3))
            state = added(block, shifted(state, 512.0, powers))
        for i in range(4):
            for k in range(3):
                ysend[i, k] = state[k]
            state = added(line(i), shifted(state, 128.0, near_powers))
        for d in (2, 1, 3):
            pltpu.make_async_remote_copy(
                src_ref=ysend.at[(z + d) % 4], dst_ref=yrecv.at[z], send_sem=n_sem.at[2], recv_sem=n_sem.at[3],
                device_id=at(2, d), device_id_type=MESH,
            ).start()
        yrecv[z] = ysend[z]

    def back_step(axis, buf, recv, ssem, rsem, own, rate):
        far = zero if axis == 0 else keep[EU]
        far, power = suffix_merge(axis, recv, rsem, far, rate)
        keep[EU] = far
        if axis < 2:
            buf[axis + 1, 0] = far
            buf[axis + 1, 1] = keep[own] + power * far
            send(axis + 1, buf, recv, ssem, rsem)
        return far

    send(0, usend, urecv, us_sem, ur_sem)
    spread_signals()

    for axis, step in enumerate(strides):
        keep[POW2 + axis] = jnp.exp(-step * rate2)
        keep[POW1 + axis] = jnp.exp(-step * keep[RATE1])

    def near(src_t, sig_t, decay):
        def body(i, st):
            t = LOCAL - 1 - i
            x0, x1, l0, l1 = st
            x1 = decay * (x1 + x0)
            x0 = decay * x0 + row(src_t, t)
            sig = row(sig_t, t)
            return x0, x1, l0 + sig * x0, l1 + sig * x1

        return lax.fori_loop(0, LOCAL, body, (zero,) * 4, unroll=UNROLL)

    unused, m2, l02, l12 = near(src2_t, sig2_t, decay2)
    keep[M2], keep[L02], keep[L12] = m2, l02, l12

    back_step(0, usend, urecv, us_sem, ur_sem, S2, POW2)
    back_step(1, usend, urecv, us_sem, ur_sem, S2, POW2)
    total_lines()
    return_signals()
    c2 = back_step(2, usend, urecv, us_sem, ur_sem, S2, POW2)
    keep[C2] = c2

    decay1 = jnp.exp(-keep[RATE1])
    decay2 = jnp.exp(-keep[RATE2])
    amp2 = keep[AMP2]

    def middle(i, st):
        t = LOCAL - 1 - i
        xa, xb = st
        xa = decay2 * xa + row(src2_t, t)
        part = jnp.sum(amp2 * xa, axis=0)
        back = part + pltpu.roll(part, 4, 0)
        here = pl.ds(pl.multiple_of(t * 8, 8), 8)
        back2_t[here, :] = back
        source = back * gain_t[here, :]
        src1_t[here, :] = source
        return xa, decay1 * xb + source[None]

    unused, s1 = lax.fori_loop(0, LOCAL, middle, (c2, zero), unroll=UNROLL)
    keep[S1] = s1
    vsend[0, 0] = s1
    send(0, vsend, vrecv, vs_sem, vr_sem)

    unused, m1, l01, l11 = near(src1_t, sig1_t, decay1)
    back_step(0, vsend, vrecv, vs_sem, vr_sem, S1, POW1)
    rate1, amp1 = keep[RATE1], keep[AMP1]
    rate2, amp2 = keep[RATE2], keep[AMP2]
    c2 = keep[C2]
    root1 = jnp.sqrt(2.0 * rate1) * SCALE
    half1, turn1 = amp1 * (0.5 * SCALE), amp1 * rate1 * SCALE
    zero_sum = keep[L02] + keep[ZA2] * c2
    one_sum = keep[L12] + keep[ZB2] * c2
    far2 = keep[M2] + (128.0 * keep[POW2 + 2]) * c2
    turn2 = amp2 * rate2 * SCALE
    grads[2] = zero_sum * jnp.sqrt(2.0 * rate2) * SCALE
    grads[3] = amp2 * (0.5 * SCALE) * zero_sum - turn2 * one_sum
    far2 = turn2 * far2
    wait_bytes(yrecv.at[pl.ds(0, 3)], n_sem.at[3])
    y1, y11, y2 = (yrecv[:, k].reshape(STATE) for k in range(3))
    zero_sum = l01 + s1 * y1
    one_sum = l11 + s1 * y11 + m1 * y1
    grads[0] = zero_sum * root1
    grads[1] = half1 * zero_sum - turn1 * one_sum
    grads[3] = grads[3] - far2 * y2

    def share(ref, q):
        return ref.at[q // 4, pl.ds((q % 4) * 2, 2)]

    for i, q in enumerate(plane):
        pltpu.make_async_remote_copy(
            src_ref=share(grads, q), dst_ref=rs_recv.at[i], send_sem=p_send.at[0], recv_sem=p_recv.at[0],
            device_id=(dp, q * 4 + z), device_id_type=MESH,
        ).start()


    back_step(1, vsend, vrecv, vs_sem, vr_sem, S1, POW1)
    outs = (value_out, key1_out, gate1_out, key2_out, gate2_out)

    def emit(i):
        pltpu.make_async_copy(made.at[i], outs[i].at[0], out_sem.at[i]).start()

    def store(i, c, tile):
        made[i, c * 128 : (c + 1) * 128, :] = tile.astype(jnp.bfloat16)

    for c in range(4):
        back = back2_t[pl.ds(c, LOCAL, stride=8), :].T
        store(2, c, back * block(2, c) * block(4, c))
        store(3, c, back * (block(3, c) * block(4, c)))
        store(4, c, block(0, c) * block(7, c))
    for i in (2, 3, 4):
        emit(i)

    wait_bytes(rs_recv, p_recv.at[0])
    total = grads[me // 4, pl.ds((me % 4) * 2, 2)]
    for i in range(15):
        total = total + rs_recv[i]
    zred[z] = total
    for d in (2, 1, 3):
        pltpu.make_async_remote_copy(
            src_ref=zred.at[z], dst_ref=zred.at[z], send_sem=p_send.at[1], recv_sem=p_recv.at[1],
            device_id=at(2, d), device_id_type=MESH,
        ).start()


    c1 = back_step(2, vsend, vrecv, vs_sem, vr_sem, S1, POW1)
    decay1 = jnp.exp(-keep[RATE1])
    amp1 = keep[AMP1]

    def last(i, xa):
        t = LOCAL - 1 - i
        xa = decay1 * xa + row(src1_t, t)
        part = jnp.sum(amp1 * xa, axis=0)
        back1_t[pl.ds(pl.multiple_of(t * 8, 8), 8), :] = part + pltpu.roll(part, 4, 0)
        return xa

    lax.fori_loop(0, LOCAL, last, c1, unroll=UNROLL)
    wait_bytes(zred.at[pl.ds(0, 3)], p_recv.at[1])
    total = (zred[0] + zred[1]) + (zred[2] + zred[3])
    piece[...] = total
    own = pltpu.make_async_copy(piece, sums_out.at[me], out_sem.at[5])
    own.start()
    for i, q in enumerate(plane):
        pltpu.make_async_remote_copy(
            src_ref=piece, dst_ref=sums_out.at[me], send_sem=p_send.at[2], recv_sem=p_recv.at[2],
            device_id=(dp, q * 4 + z), device_id_type=MESH,
        ).start()

    for c in range(4):
        back = back1_t[pl.ds(c, LOCAL, stride=8), :].T
        store(0, c, back * block(5, c))
        store(1, c, back * block(6, c))
    for i in (0, 1):
        emit(i)

    wait_bytes(sums_out.at[pl.ds(0, 15)], p_recv.at[2])
    for axis in range(3):
        departed(axis, urecv, us_sem)
        departed(axis, vrecv, vs_sem)
    wait_bytes(nrecv.at[pl.ds(0, 3)], n_sem.at[0])
    wait_bytes(yrecv.at[pl.ds(0, 3)], n_sem.at[2])
    for k in range(1, 16):
        @pl.when(me + k < 16)
        def _():
            wait_bytes(tsend, ts_sem.at[k - 1])
    wait_bytes(rs_recv, p_send.at[0])
    wait_bytes(zred.at[pl.ds(0, 3)], p_send.at[1])
    wait_bytes(rs_recv, p_send.at[2])
    for i in range(5):
        pltpu.make_async_copy(made.at[i], outs[i].at[0], out_sem.at[i]).wait()
    own.wait()


def hand_over(*refs):
    made, sums, outs, held, turned, thin, sem_in, sem_out = refs[:5], refs[5], refs[6:15], *refs[15:]
    rows = CHAN // CUTS
    loads, stores = [], []
    for i in range(5):
        for j in range(CUTS):
            here = (i, 0, pl.ds(j * rows, rows))
            there = (0, pl.ds(j * rows, rows))
            loads.append(pltpu.make_async_copy(made[i].at[there], held.at[here], sem_in.at[len(loads)]))
            stores.append(pltpu.make_async_copy(held.at[here], outs[i].at[there], sem_out.at[len(stores)]))
    last = pltpu.make_async_copy(sums, turned, sem_in.at[len(loads)])
    last.start()
    for load in loads:
        load.start()
    last.wait()
    for i in range(4):
        for c in range(4):
            thin[i, :, c * 128 : (c + 1) * 128] = turned[pl.ds(i * 64 + c, ORDER, stride=4), :]
        stores.append(pltpu.make_async_copy(thin.at[i], outs[5 + i], sem_out.at[len(stores)]))
        stores[-1].start()
    for load, store in zip(loads, stores):
        load.wait()
        store.start()
    for store in stores:
        store.wait()


def per_device(
    value, key_one, gate_one, conv_one, key_two, gate_two, conv_two, grad_out,
    residues_one, log_rate_one, residues_two, log_rate_two,
):
    f32 = jnp.float32
    vmem = pltpu.VMEM
    dma = pltpu.SemaphoreType.DMA
    turned = vmem((LOCAL * 8, 128), f32)
    bf16 = jnp.bfloat16
    shape = value.shape
    anywhere = pl.BlockSpec(memory_space=pl.ANY)
    made = pl.pallas_call(
        kernel,
        out_shape=[jax.ShapeDtypeStruct(shape, bf16)] * 5 + [jax.ShapeDtypeStruct((16, 2, 8, 128), f32)],
        in_specs=[anywhere] * 12,
        out_specs=[anywhere] * 6,
        scratch_shapes=[
            vmem((8, CHAN, LOCAL), bf16),
            vmem((4, ORDER, CHAN), f32),
            vmem((5, CHAN, LOCAL), bf16),
            dma((12,)),
            turned, turned, turned, turned, turned, turned, turned,
            vmem((4, 64, 128), f32),
            vmem((19,) + STATE, f32),
            vmem((3, 2) + STATE, f32),
            vmem((3, 3) + STATE, f32),
            vmem((4, 3, 2, 8, 128), f32),
            vmem((4, 3, 2, 8, 128), f32),
            vmem((3, 2, 8, 128), f32),
            vmem((15, 3, 2, 8, 128), f32),
            vmem((4, 3, 2, 8, 128), f32),
            vmem((4, 3, 2, 8, 128), f32),
            vmem((3, 2) + STATE, f32),
            vmem((3, 3) + STATE, f32),
            vmem((4,) + STATE, f32),
            vmem((15, 2, 8, 128), f32),
            vmem((4, 2, 8, 128), f32),
            vmem((2, 8, 128), f32),
            dma((5,)), dma((5,)), dma((4,)), dma((15,)), dma((15,)), dma((5,)), dma((5,)), dma((3,)), dma((3,)), dma((6,)),
        ],
        compiler_params=pltpu.CompilerParams(
            collective_id=0, has_side_effects=True, vmem_limit_bytes=56 * 1024 * 1024
        ),
        name="hyena_back",
    )(
        value, key_one, gate_one, conv_one, key_two, gate_two, conv_two, grad_out,
        residues_one.T, log_rate_one.T, residues_two.T, log_rate_two.T,
    )
    made = list(made[:5]) + [made[5].reshape(4 * ORDER * 4, 128)]
    thin = jax.ShapeDtypeStruct((ORDER, CHAN), f32)
    outs = pl.pallas_call(
        hand_over,
        out_shape=[jax.ShapeDtypeStruct(shape, bf16)] * 5 + [thin] * 4,
        in_specs=[anywhere] * 6,
        out_specs=[anywhere] * 9,
        scratch_shapes=[
            vmem((5,) + shape, bf16),
            vmem((4 * ORDER * 4, 128), f32),
            vmem((4, ORDER, CHAN), f32),
            dma((5 * CUTS + 1,)),
            dma((5 * CUTS + 4,)),
        ],
        name="hand_over",
    )(*made)
    return tuple(outs[:5]) + tuple(out.T for out in outs[5:])


def solution(mesh):
    wide = P(None, "dp", "context")
    thin = P("dp", None)
    return jax.shard_map(
        per_device,
        mesh=mesh,
        in_specs=(wide,) * 8 + (thin,) * 4,
        out_specs=(wide,) * 5 + (thin,) * 4,
        check_vma=False,
    )
```

```python
import math

import jax
import jax.numpy as jnp
from jax import lax
from jax.experimental import pallas as pl
from jax.experimental.pallas import tpu as pltpu
from jax.sharding import PartitionSpec as P

MESH = pl.DeviceIdType.MESH
LOCAL = 128
CHAN = 512
ORDER = 16
STATE = (8, 8, 128)
SCALE = 1.0 / math.sqrt(8192.0)
UNROLL = 8

(AMP1, RATE1, AMP2, RATE2, S2, M2, L02, L12, ZA2, ZB2, C2, S1, EU, POW1, POW2) = (*range(13), 13, 16)


def wait_bytes(ref, sem):
    pltpu.make_async_copy(ref, ref, sem).wait()


def kernel(
    value, key_one, gate_one, conv_one, key_two, gate_two, conv_two, grad_out, res1, lr1, res2, lr2,
    value_out, key1_out, gate1_out, key2_out, gate2_out, sums_out,
    wide, narrow, in_sem, src2_t, gain_t, sig1_t, sig2_t, src1_t, back2_t, back1_t, par,
    keep, usend, urecv, nsend, nrecv, tsend, trecv, ysend, yrecv, vsend, vrecv, grads, rs_recv, zred, piece,
    us_sem, ur_sem, n_sem, ts_sem, tr_sem, vs_sem, vr_sem, p_send, p_recv,
):
    dp = lax.axis_index("dp")
    ctx = lax.axis_index("context")
    y, x, z = ctx // 16, (ctx // 4) % 4, ctx % 4
    me = ctx // 4
    coords = (y, x, z)

    def at(axis, d):
        if axis == 0:
            return (dp, ((y + d) % 4) * 16 + x * 4 + z)
        if axis == 1:
            return (dp, y * 16 + ((x + d) % 4) * 4 + z)
        return (dp, y * 16 + x * 4 + (z + d) % 4)

    plane = [
        (((y + e) % 4) * 4 + (x + f) % 4) for e in (2, 1, 3, 0) for f in (2, 1, 3, 0) if e or f
    ]

    barrier = pltpu.get_barrier_semaphore()
    for d in (2, 1, 3):
        pl.semaphore_signal(barrier, inc=1, device_id=at(2, d), device_id_type=MESH)

    trecv[...] = jnp.zeros(trecv.shape, jnp.float32)
    urecv[0] = jnp.zeros(urecv.shape[1:], jnp.float32)
    vrecv[0] = jnp.zeros(vrecv.shape[1:], jnp.float32)

    for axis in (0, 1):
        for d in (2, 1, 3):
            pl.semaphore_signal(barrier, inc=1, device_id=at(axis, d), device_id_type=MESH)

    wide_in = (grad_out, gate_two, key_two, gate_one, conv_one, key_one, value, conv_two)
    narrow_in = (lr2, lr1, res2, res1)
    loads = []
    for i, ref in enumerate(narrow_in):
        loads.append(pltpu.make_async_copy(ref, narrow.at[i], in_sem.at[8 + i]))
    for i, ref in enumerate(wide_in):
        loads.append(pltpu.make_async_copy(ref.at[0], wide.at[i], in_sem.at[i]))
    for load in loads:
        load.start()

    for i in range(4):
        loads[i].wait()
        for c in range(4):
            par[i, pl.ds(c, ORDER, stride=4), :] = narrow[i, :, c * 128 : (c + 1) * 128]
    rate2 = jnp.exp(par[0]).reshape(STATE)
    rate1 = jnp.exp(par[1]).reshape(STATE)
    keep[RATE2] = rate2
    keep[RATE1] = rate1
    keep[AMP2] = par[2].reshape(STATE) * jnp.sqrt(2.0 * rate2)
    keep[AMP1] = par[3].reshape(STATE) * jnp.sqrt(2.0 * rate1)

    def block(i, c):
        return wide[i, c * 128 : (c + 1) * 128, :].astype(jnp.float32)

    def put(ref, c, tile):
        flipped = tile.T
        ref[pl.ds(c, LOCAL, stride=8), :] = flipped
        ref[pl.ds(c + 4, LOCAL, stride=8), :] = flipped

    def row(ref, t):
        return ref[pl.ds(pl.multiple_of(t * 8, 8), 8), :][None]

    zero = jnp.zeros(STATE, jnp.float32)

    loads[4].wait()
    loads[5].wait()
    for c in range(4):
        put(src2_t, c, block(0, c) * block(1, c))

    decay2 = jnp.exp(-rate2)

    def first(i, state):
        return decay2 * state + row(src2_t, LOCAL - 1 - i)

    state = lax.fori_loop(0, LOCAL, first, zero, unroll=UNROLL)
    keep[S2] = state
    usend[0, 0] = state

    for i in range(6, 12):
        loads[i].wait()
    for c in range(4):
        kt, go = block(2, c), block(3, c)
        put(gain_t, c, kt * go)
        put(sig2_t, c, kt * (go * block(4, c)))
        put(sig1_t, c, block(5, c) * block(6, c))

    decay1 = jnp.exp(-keep[RATE1])

    def ahead(t, st):
        a0, a1, b0, b1 = st
        u = a0 + row(sig1_t, t)
        v = b0 + row(sig2_t, t)
        return decay1 * u, decay1 * (a1 + u), decay2 * v, decay2 * (b1 + v)

    za1, zb1, za2, zb2 = lax.fori_loop(0, LOCAL, ahead, (zero,) * 4, unroll=UNROLL)
    keep[ZA2], keep[ZB2] = za2, zb2
    for k, array in enumerate((za1, zb1, za2)):
        nsend[:, k] = array.reshape(4, 2, 8, 128)

    pl.semaphore_wait(barrier, 9)

    def send(axis, buf, recv, ssem, rsem):
        for d in (2, 1, 3):
            copy = pltpu.make_async_remote_copy(
                src_ref=buf.at[axis, 0 if axis == 0 else (coords[axis] + d) // 4],
                dst_ref=recv.at[axis, 3 - d],
                send_sem=ssem.at[d - 1 if axis == 0 else axis + 2],
                recv_sem=rsem.at[3 - d if axis == 0 else axis + 2],
                device_id=at(axis, d),
                device_id_type=MESH,
            )
            if axis:
                copy.start()
            else:
                pl.when(y + d >= 4)(copy.start)

    def arrived(axis, recv, rsem):
        if axis:
            wait_bytes(recv.at[axis], rsem.at[axis + 2])
        else:
            for d in (1, 2, 3):
                @pl.when(y + d < 4)
                def _():
                    wait_bytes(recv.at[0, d - 1], rsem.at[d - 1])

    def departed(axis, recv, ssem):
        if axis:
            wait_bytes(recv.at[axis], ssem.at[axis + 2])
        else:
            for d in (1, 2, 3):
                @pl.when(y + d >= 4)
                def _():
                    wait_bytes(recv.at[0, d - 1], ssem.at[d - 1])

    strides = (2048.0, 512.0, 128.0)

    def suffix_merge(axis, recv, rsem, far, rate):
        arrived(axis, recv, rsem)
        power = keep[rate + axis]
        for d in (3, 2, 1):
            far = recv[axis, d - 1] + power * far
        return far, power

    def spread_signals():
        for d in (2, 1, 3):
            pltpu.make_async_remote_copy(
                src_ref=nsend.at[(z + d) % 4], dst_ref=nrecv.at[z], send_sem=n_sem.at[0], recv_sem=n_sem.at[1],
                device_id=at(2, d), device_id_type=MESH,
            ).start()
        nrecv[z] = nsend[z]

    def quarter_rates():
        return keep[RATE1, pl.ds(2 * z, 2)], keep[RATE2, pl.ds(2 * z, 2)]

    def shifted(state, length, powers):
        f0, f1, f2 = state
        return powers[0] * f0, powers[0] * (f1 + length * f0), powers[1] * f2

    def added(left, right):
        return tuple(p + q for p, q in zip(left, right))

    def line(i):
        return tuple(nrecv[i, k] for k in range(3))

    def total_lines():
        wait_bytes(nrecv.at[pl.ds(0, 3)], n_sem.at[1])
        powers = tuple(jnp.exp(-128.0 * rate) for rate in quarter_rates())
        state = line(0)
        for i in (1, 2, 3):
            state = added(line(i), shifted(state, 128.0, powers))
        for k in range(3):
            tsend[k] = state[k]
        for k in range(15, 0, -1):
            @pl.when(me + k < 16)
            def _():
                pltpu.make_async_remote_copy(
                    src_ref=tsend, dst_ref=trecv.at[k - 1], send_sem=ts_sem.at[k - 1], recv_sem=tr_sem.at[k - 1],
                    device_id=(dp, (me + k) * 4 + z), device_id_type=MESH,
                ).start()


    def return_signals():
        near_powers = []
        powers = []
        for rate in quarter_rates():
            powers.append(jnp.exp(-512.0 * rate))
            near_powers.append(jnp.exp(-128.0 * rate))
        for k in range(1, 16):
            @pl.when(me >= k)
            def _():
                wait_bytes(trecv.at[k - 1], tr_sem.at[k - 1])
        state = tuple(jnp.zeros((2, 8, 128), jnp.float32) for _ in range(3))
        for k in range(15, 0, -1):
            block = tuple(trecv[k - 1, i] for i in range(3))
            state = added(block, shifted(state, 512.0, powers))
        for i in range(4):
            for k in range(3):
                ysend[i, k] = state[k]
            state = added(line(i), shifted(state, 128.0, near_powers))
        for d in (2, 1, 3):
            pltpu.make_async_remote_copy(
                src_ref=ysend.at[(z + d) % 4], dst_ref=yrecv.at[z], send_sem=n_sem.at[2], recv_sem=n_sem.at[3],
                device_id=at(2, d), device_id_type=MESH,
            ).start()
        yrecv[z] = ysend[z]

    def back_step(axis, buf, recv, ssem, rsem, own, rate):
        far = zero if axis == 0 else keep[EU]
        far, power = suffix_merge(axis, recv, rsem, far, rate)
        keep[EU] = far
        if axis < 2:
            buf[axis + 1, 0] = far
            buf[axis + 1, 1] = keep[own] + power * far
            send(axis + 1, buf, recv, ssem, rsem)
        return far

    spread_signals()
    send(0, usend, urecv, us_sem, ur_sem)

    for axis, step in enumerate(strides):
        keep[POW2 + axis] = jnp.exp(-step * rate2)
        keep[POW1 + axis] = jnp.exp(-step * keep[RATE1])

    def near(src_t, sig_t, decay):
        def body(i, st):
            t = LOCAL - 1 - i
            x0, x1, l0, l1 = st
            x1 = decay * (x1 + x0)
            x0 = decay * x0 + row(src_t, t)
            sig = row(sig_t, t)
            return x0, x1, l0 + sig * x0, l1 + sig * x1

        return lax.fori_loop(0, LOCAL, body, (zero,) * 4, unroll=UNROLL)

    unused, m2, l02, l12 = near(src2_t, sig2_t, decay2)
    keep[M2], keep[L02], keep[L12] = m2, l02, l12

    back_step(0, usend, urecv, us_sem, ur_sem, S2, POW2)
    back_step(1, usend, urecv, us_sem, ur_sem, S2, POW2)
    total_lines()
    return_signals()
    c2 = back_step(2, usend, urecv, us_sem, ur_sem, S2, POW2)
    keep[C2] = c2

    decay1 = jnp.exp(-keep[RATE1])
    decay2 = jnp.exp(-keep[RATE2])
    amp2 = keep[AMP2]

    def middle(i, st):
        t = LOCAL - 1 - i
        xa, xb = st
        xa = decay2 * xa + row(src2_t, t)
        part = jnp.sum(amp2 * xa, axis=0)
        back = part + pltpu.roll(part, 4, 0)
        here = pl.ds(pl.multiple_of(t * 8, 8), 8)
        back2_t[here, :] = back
        source = back * gain_t[here, :]
        src1_t[here, :] = source
        return xa, decay1 * xb + source[None]

    unused, s1 = lax.fori_loop(0, LOCAL, middle, (c2, zero), unroll=UNROLL)
    keep[S1] = s1
    vsend[0, 0] = s1
    send(0, vsend, vrecv, vs_sem, vr_sem)

    unused, m1, l01, l11 = near(src1_t, sig1_t, decay1)
    back_step(0, vsend, vrecv, vs_sem, vr_sem, S1, POW1)
    rate1, amp1 = keep[RATE1], keep[AMP1]
    rate2, amp2 = keep[RATE2], keep[AMP2]
    c2 = keep[C2]
    root1 = jnp.sqrt(2.0 * rate1) * SCALE
    half1, turn1 = amp1 * (0.5 * SCALE), amp1 * rate1 * SCALE
    zero_sum = keep[L02] + keep[ZA2] * c2
    one_sum = keep[L12] + keep[ZB2] * c2
    far2 = keep[M2] + (128.0 * keep[POW2 + 2]) * c2
    turn2 = amp2 * rate2 * SCALE
    grads[2] = zero_sum * jnp.sqrt(2.0 * rate2) * SCALE
    grads[3] = amp2 * (0.5 * SCALE) * zero_sum - turn2 * one_sum
    far2 = turn2 * far2
    wait_bytes(yrecv.at[pl.ds(0, 3)], n_sem.at[3])
    y1, y11, y2 = (yrecv[:, k].reshape(STATE) for k in range(3))
    zero_sum = l01 + s1 * y1
    one_sum = l11 + s1 * y11 + m1 * y1
    grads[0] = zero_sum * root1
    grads[1] = half1 * zero_sum - turn1 * one_sum
    grads[3] = grads[3] - far2 * y2

    def share(ref, q):
        return ref.at[q // 4, pl.ds((q % 4) * 2, 2)]

    for i, q in enumerate(plane):
        pltpu.make_async_remote_copy(
            src_ref=share(grads, q), dst_ref=rs_recv.at[i], send_sem=p_send.at[0], recv_sem=p_recv.at[0],
            device_id=(dp, q * 4 + z), device_id_type=MESH,
        ).start()


    back_step(1, vsend, vrecv, vs_sem, vr_sem, S1, POW1)
    wait_bytes(rs_recv, p_recv.at[0])
    total = grads[me // 4, pl.ds((me % 4) * 2, 2)]
    for i in range(15):
        total = total + rs_recv[i]
    zred[z] = total
    for d in (2, 1, 3):
        pltpu.make_async_remote_copy(
            src_ref=zred.at[z], dst_ref=zred.at[z], send_sem=p_send.at[1], recv_sem=p_recv.at[1],
            device_id=at(2, d), device_id_type=MESH,
        ).start()

    outs = (value_out, key1_out, gate1_out, key2_out, gate2_out)

    def store(i, c, tile):
        outs[i][0, c * 128 : (c + 1) * 128, :] = tile.astype(jnp.bfloat16)

    for c in range(4):
        back = back2_t[pl.ds(c, LOCAL, stride=8), :].T
        store(2, c, back * block(2, c) * block(4, c))
        store(3, c, back * (block(3, c) * block(4, c)))
        store(4, c, block(0, c) * block(7, c))


    wait_bytes(zred.at[pl.ds(0, 3)], p_recv.at[1])
    total = (zred[0] + zred[1]) + (zred[2] + zred[3])
    piece[...] = total
    sums_out[me] = total
    for i, q in enumerate(plane):
        pltpu.make_async_remote_copy(
            src_ref=piece, dst_ref=sums_out.at[me], send_sem=p_send.at[2], recv_sem=p_recv.at[2],
            device_id=(dp, q * 4 + z), device_id_type=MESH,
        ).start()

    c1 = back_step(2, vsend, vrecv, vs_sem, vr_sem, S1, POW1)
    decay1 = jnp.exp(-keep[RATE1])
    amp1 = keep[AMP1]

    def last(i, xa):
        t = LOCAL - 1 - i
        xa = decay1 * xa + row(src1_t, t)
        part = jnp.sum(amp1 * xa, axis=0)
        back1_t[pl.ds(pl.multiple_of(t * 8, 8), 8), :] = part + pltpu.roll(part, 4, 0)
        return xa

    lax.fori_loop(0, LOCAL, last, c1, unroll=UNROLL)
    for c in range(4):
        back = back1_t[pl.ds(c, LOCAL, stride=8), :].T
        store(0, c, back * block(5, c))
        store(1, c, back * block(6, c))

    wait_bytes(sums_out.at[pl.ds(0, 15)], p_recv.at[2])
    for axis in range(3):
        departed(axis, urecv, us_sem)
        departed(axis, vrecv, vs_sem)
    wait_bytes(nrecv.at[pl.ds(0, 3)], n_sem.at[0])
    wait_bytes(yrecv.at[pl.ds(0, 3)], n_sem.at[2])
    for k in range(1, 16):
        @pl.when(me + k < 16)
        def _():
            wait_bytes(tsend, ts_sem.at[k - 1])
    wait_bytes(rs_recv, p_send.at[0])
    wait_bytes(zred.at[pl.ds(0, 3)], p_send.at[1])
    wait_bytes(rs_recv, p_send.at[2])


def hand_over(*refs):
    made, turned, outs, thin, sem = refs[:5], refs[5], refs[6:15], *refs[15:]
    stores = [pltpu.make_async_copy(made[i], outs[i], sem.at[i]) for i in range(5)]
    stores += [pltpu.make_async_copy(thin.at[i], outs[5 + i], sem.at[5 + i]) for i in range(4)]
    for store in stores[:5]:
        store.start()
    for i in range(4):
        for c in range(4):
            thin[i, :, c * 128 : (c + 1) * 128] = turned[pl.ds(i * 64 + c, ORDER, stride=4), :]
        stores[5 + i].start()
    for store in stores:
        store.wait()


def per_device(
    value, key_one, gate_one, conv_one, key_two, gate_two, conv_two, grad_out,
    residues_one, log_rate_one, residues_two, log_rate_two,
):
    f32 = jnp.float32
    vmem = pltpu.VMEM
    dma = pltpu.SemaphoreType.DMA
    turned = vmem((LOCAL * 8, 128), f32)
    bf16 = jnp.bfloat16
    shape = value.shape
    anywhere = pl.BlockSpec(memory_space=pl.ANY)
    inside = pl.BlockSpec(memory_space=pltpu.VMEM)
    made = pl.pallas_call(
        kernel,
        out_shape=[vmem(shape, bf16)] * 5 + [vmem((16, 2, 8, 128), f32)],
        in_specs=[anywhere] * 12,
        out_specs=[inside] * 6,
        scratch_shapes=[
            vmem((8, CHAN, LOCAL), bf16),
            vmem((4, ORDER, CHAN), f32),
            dma((12,)),
            turned, turned, turned, turned, turned, turned, turned,
            vmem((4, 64, 128), f32),
            vmem((19,) + STATE, f32),
            vmem((3, 2) + STATE, f32),
            vmem((3, 3) + STATE, f32),
            vmem((4, 3, 2, 8, 128), f32),
            vmem((4, 3, 2, 8, 128), f32),
            vmem((3, 2, 8, 128), f32),
            vmem((15, 3, 2, 8, 128), f32),
            vmem((4, 3, 2, 8, 128), f32),
            vmem((4, 3, 2, 8, 128), f32),
            vmem((3, 2) + STATE, f32),
            vmem((3, 3) + STATE, f32),
            vmem((4,) + STATE, f32),
            vmem((15, 2, 8, 128), f32),
            vmem((4, 2, 8, 128), f32),
            vmem((2, 8, 128), f32),
            dma((5,)), dma((5,)), dma((4,)), dma((15,)), dma((15,)), dma((5,)), dma((5,)), dma((3,)), dma((3,)),
        ],
        compiler_params=pltpu.CompilerParams(
            collective_id=0, has_side_effects=True, vmem_limit_bytes=56 * 1024 * 1024
        ),
        name="hyena_back",
    )(
        value, key_one, gate_one, conv_one, key_two, gate_two, conv_two, grad_out,
        residues_one.T, log_rate_one.T, residues_two.T, log_rate_two.T,
    )
    made = list(made[:5]) + [made[5].reshape(4 * ORDER * 4, 128)]
    thin = jax.ShapeDtypeStruct((ORDER, CHAN), f32)
    outs = pl.pallas_call(
        hand_over,
        out_shape=[jax.ShapeDtypeStruct(shape, bf16)] * 5 + [thin] * 4,
        in_specs=[inside] * 6,
        out_specs=[anywhere] * 9,
        scratch_shapes=[
            vmem((4, ORDER, CHAN), f32),
            dma((9,)),
        ],
        name="hand_over",
    )(*(pltpu.with_memory_space_constraint(array, pltpu.VMEM) for array in made))
    return tuple(outs[:5]) + tuple(out.T for out in outs[5:])


def solution(mesh):
    wide = P(None, "dp", "context")
    thin = P("dp", None)
    return jax.shard_map(
        per_device,
        mesh=mesh,
        in_specs=(wide,) * 8 + (thin,) * 4,
        out_specs=(wide,) * 5 + (thin,) * 4,
        check_vma=False,
    )
```

```python
import math

import jax
import jax.numpy as jnp
from jax import lax
from jax.experimental import pallas as pl
from jax.experimental.pallas import tpu as pltpu
from jax.sharding import PartitionSpec as P

MESH = pl.DeviceIdType.MESH
LOCAL = 128
CHAN = 512
ORDER = 16
STATE = (8, 8, 128)
HALF = (4, 8, 128)
SCALE = 1.0 / math.sqrt(8192.0)
UNROLL = 8

(AMP1, RATE1, AMP2, RATE2, S2, M2, L02, L12, ZA2, ZB2, C2, S1, EU, POW1, POW2) = (*range(13), 13, 16)


def wait_bytes(ref, sem):
    pltpu.make_async_copy(ref, ref, sem).wait()


def kernel(
    value, key_one, gate_one, conv_one, key_two, gate_two, conv_two, grad_out, res1, lr1, res2, lr2,
    value_out, key1_out, gate1_out, key2_out, gate2_out, sums_out,
    wide, narrow, in_sem, src2_t, gain_t, sig1_t, sig2_t, src1_t, back2_t, back1_t, par,
    keep, usend, urecv, nsend, nrecv, tsend, trecv, ysend, yrecv, vsend, vrecv, grads, rs_recv, zred, piece,
    us_sem, ur_sem, n_sem, ts_sem, tr_sem, vs_sem, vr_sem, p_send, p_recv,
):
    dp = lax.axis_index("dp")
    ctx = lax.axis_index("context")
    y, x, z = ctx // 16, (ctx // 4) % 4, ctx % 4
    me = ctx // 4
    coords = (y, x, z)

    def at(axis, d):
        if axis == 0:
            return (dp, ((y + d) % 4) * 16 + x * 4 + z)
        if axis == 1:
            return (dp, y * 16 + ((x + d) % 4) * 4 + z)
        return (dp, y * 16 + x * 4 + (z + d) % 4)

    plane = [
        (((y + e) % 4) * 4 + (x + f) % 4) for e in (2, 1, 3, 0) for f in (2, 1, 3, 0) if e or f
    ]

    barrier = pltpu.get_barrier_semaphore()
    for d in (2, 1, 3):
        pl.semaphore_signal(barrier, inc=1, device_id=at(2, d), device_id_type=MESH)

    trecv[...] = jnp.zeros(trecv.shape, jnp.float32)
    for h in range(2):
        urecv[h, 0] = jnp.zeros(urecv.shape[2:], jnp.float32)
        vrecv[h, 0] = jnp.zeros(vrecv.shape[2:], jnp.float32)

    for axis in (0, 1):
        for d in (2, 1, 3):
            pl.semaphore_signal(barrier, inc=1, device_id=at(axis, d), device_id_type=MESH)

    wide_in = (grad_out, gate_two, key_two, gate_one, conv_one, key_one, value, conv_two)
    narrow_in = (lr2, lr1, res2, res1)
    loads = []
    for i, ref in enumerate(narrow_in):
        loads.append(pltpu.make_async_copy(ref, narrow.at[i], in_sem.at[8 + i]))
    for i, ref in enumerate(wide_in):
        loads.append(pltpu.make_async_copy(ref.at[0], wide.at[i], in_sem.at[i]))
    for load in loads:
        load.start()

    for i in range(4):
        loads[i].wait()
        for c in range(4):
            par[i, pl.ds(c, ORDER, stride=4), :] = narrow[i, :, c * 128 : (c + 1) * 128]
    rate2 = jnp.exp(par[0]).reshape(STATE)
    rate1 = jnp.exp(par[1]).reshape(STATE)
    keep[RATE2] = rate2
    keep[RATE1] = rate1
    keep[AMP2] = par[2].reshape(STATE) * jnp.sqrt(2.0 * rate2)
    keep[AMP1] = par[3].reshape(STATE) * jnp.sqrt(2.0 * rate1)

    def block(i, c):
        return wide[i, c * 128 : (c + 1) * 128, :].astype(jnp.float32)

    def put(ref, c, tile):
        flipped = tile.T
        ref[pl.ds(c, LOCAL, stride=8), :] = flipped
        ref[pl.ds(c + 4, LOCAL, stride=8), :] = flipped

    def row(ref, t):
        return ref[pl.ds(pl.multiple_of(t * 8, 8), 8), :][None]

    zero = jnp.zeros(STATE, jnp.float32)

    loads[4].wait()
    loads[5].wait()
    for c in range(4):
        put(src2_t, c, block(0, c) * block(1, c))

    decay2 = jnp.exp(-rate2)

    def first(i, state):
        return decay2 * state + row(src2_t, LOCAL - 1 - i)

    state = lax.fori_loop(0, LOCAL, first, zero, unroll=UNROLL)
    keep[S2] = state

    for i in range(6, 12):
        loads[i].wait()
    for c in range(4):
        kt, go = block(2, c), block(3, c)
        put(gain_t, c, kt * go)
        put(sig2_t, c, kt * (go * block(4, c)))
        put(sig1_t, c, block(5, c) * block(6, c))

    decay1 = jnp.exp(-keep[RATE1])

    def ahead(t, st):
        a0, a1, b0, b1 = st
        u = a0 + row(sig1_t, t)
        v = b0 + row(sig2_t, t)
        return decay1 * u, decay1 * (a1 + u), decay2 * v, decay2 * (b1 + v)

    za1, zb1, za2, zb2 = lax.fori_loop(0, LOCAL, ahead, (zero,) * 4, unroll=UNROLL)
    keep[ZA2], keep[ZB2] = za2, zb2
    for k, array in enumerate((za1, zb1, za2)):
        nsend[:, k] = array.reshape(4, 2, 8, 128)

    pl.semaphore_wait(barrier, 9)

    def send(axis, buf, recv, ssem, rsem, h):
        for d in (2, 1, 3):
            copy = pltpu.make_async_remote_copy(
                src_ref=buf.at[h, axis, 0 if axis == 0 else (coords[axis] + d) // 4],
                dst_ref=recv.at[h, axis, 3 - d],
                send_sem=ssem.at[5 * h + (d - 1 if axis == 0 else axis + 2)],
                recv_sem=rsem.at[5 * h + (3 - d if axis == 0 else axis + 2)],
                device_id=at(axis, d),
                device_id_type=MESH,
            )
            if axis:
                copy.start()
            else:
                pl.when(y + d >= 4)(copy.start)

    def arrived(axis, recv, rsem, h):
        if axis:
            wait_bytes(recv.at[h, axis], rsem.at[5 * h + axis + 2])
        else:
            for d in (1, 2, 3):
                @pl.when(y + d < 4)
                def _():
                    wait_bytes(recv.at[h, 0, d - 1], rsem.at[5 * h + d - 1])

    def departed(axis, recv, ssem, h):
        if axis:
            wait_bytes(recv.at[h, axis], ssem.at[5 * h + axis + 2])
        else:
            for d in (1, 2, 3):
                @pl.when(y + d >= 4)
                def _():
                    wait_bytes(recv.at[h, 0, d - 1], ssem.at[5 * h + d - 1])

    strides = (2048.0, 512.0, 128.0)

    def spread_signals():
        for d in (2, 1, 3):
            pltpu.make_async_remote_copy(
                src_ref=nsend.at[(z + d) % 4], dst_ref=nrecv.at[z], send_sem=n_sem.at[0], recv_sem=n_sem.at[1],
                device_id=at(2, d), device_id_type=MESH,
            ).start()
        nrecv[z] = nsend[z]

    def quarter_rates():
        return keep[RATE1, pl.ds(2 * z, 2)], keep[RATE2, pl.ds(2 * z, 2)]

    def shifted(state, length, powers):
        f0, f1, f2 = state
        return powers[0] * f0, powers[0] * (f1 + length * f0), powers[1] * f2

    def added(left, right):
        return tuple(p + q for p, q in zip(left, right))

    def line(i):
        return tuple(nrecv[i, k] for k in range(3))

    def total_lines():
        wait_bytes(nrecv.at[pl.ds(0, 3)], n_sem.at[1])
        powers = tuple(jnp.exp(-128.0 * rate) for rate in quarter_rates())
        state = line(0)
        for i in (1, 2, 3):
            state = added(line(i), shifted(state, 128.0, powers))
        for k in range(3):
            tsend[k] = state[k]
        for k in (10, 6, 9, 14, 11, 7, 5, 13, 2, 8, 3, 15, 4, 1, 12):
            @pl.when(me + k < 16)
            def _():
                pltpu.make_async_remote_copy(
                    src_ref=tsend, dst_ref=trecv.at[k - 1], send_sem=ts_sem.at[k - 1], recv_sem=tr_sem.at[k - 1],
                    device_id=(dp, (me + k) * 4 + z), device_id_type=MESH,
                ).start()


    def return_signals():
        near_powers = []
        powers = []
        for rate in quarter_rates():
            powers.append(jnp.exp(-512.0 * rate))
            near_powers.append(jnp.exp(-128.0 * rate))
        for k in range(1, 16):
            @pl.when(me >= k)
            def _():
                wait_bytes(trecv.at[k - 1], tr_sem.at[k - 1])
        state = tuple(jnp.zeros((2, 8, 128), jnp.float32) for _ in range(3))
        for k in range(15, 0, -1):
            block = tuple(trecv[k - 1, i] for i in range(3))
            state = added(block, shifted(state, 512.0, powers))
        for i in range(4):
            for k in range(3):
                ysend[i, k] = state[k]
            state = added(line(i), shifted(state, 128.0, near_powers))
        for d in (2, 1, 3):
            pltpu.make_async_remote_copy(
                src_ref=ysend.at[(z + d) % 4], dst_ref=yrecv.at[z], send_sem=n_sem.at[2], recv_sem=n_sem.at[3],
                device_id=at(2, d), device_id_type=MESH,
            ).start()
        yrecv[z] = ysend[z]

    def back_step(axis, buf, recv, ssem, rsem, own, power):
        for h in range(2):
            part = pl.ds(4 * h, 4)
            arrived(axis, recv, rsem, h)
            scale = keep[power + axis, part]
            far = recv[h, axis, 2]
            if axis:
                far = far + scale * keep[EU, part]
            for d in (2, 1):
                far = recv[h, axis, d - 1] + scale * far
            keep[EU, part] = far
            if axis < 2:
                buf[h, axis + 1, 0] = far
                buf[h, axis + 1, 1] = keep[own, part] + scale * far
                send(axis + 1, buf, recv, ssem, rsem, h)
        return keep[EU]

    def begin(state, buf, recv, ssem, rsem):
        for h in range(2):
            buf[h, 0, 0] = state[4 * h : 4 * h + 4]
            send(0, buf, recv, ssem, rsem, h)

    spread_signals()
    begin(keep[S2], usend, urecv, us_sem, ur_sem)

    for axis, step in enumerate(strides):
        keep[POW2 + axis] = jnp.exp(-step * rate2)
        keep[POW1 + axis] = jnp.exp(-step * keep[RATE1])

    def near(src_t, sig_t, decay):
        def body(i, st):
            t = LOCAL - 1 - i
            x0, x1, l0, l1 = st
            x1 = decay * (x1 + x0)
            x0 = decay * x0 + row(src_t, t)
            sig = row(sig_t, t)
            return x0, x1, l0 + sig * x0, l1 + sig * x1

        return lax.fori_loop(0, LOCAL, body, (zero,) * 4, unroll=UNROLL)

    unused, m2, l02, l12 = near(src2_t, sig2_t, decay2)
    keep[M2], keep[L02], keep[L12] = m2, l02, l12

    back_step(0, usend, urecv, us_sem, ur_sem, S2, POW2)
    back_step(1, usend, urecv, us_sem, ur_sem, S2, POW2)
    total_lines()
    return_signals()
    c2 = back_step(2, usend, urecv, us_sem, ur_sem, S2, POW2)
    keep[C2] = c2

    decay1 = jnp.exp(-keep[RATE1])
    decay2 = jnp.exp(-keep[RATE2])
    amp2 = keep[AMP2]

    def middle(i, st):
        t = LOCAL - 1 - i
        xa, xb = st
        xa = decay2 * xa + row(src2_t, t)
        part = jnp.sum(amp2 * xa, axis=0)
        back = part + pltpu.roll(part, 4, 0)
        here = pl.ds(pl.multiple_of(t * 8, 8), 8)
        back2_t[here, :] = back
        source = back * gain_t[here, :]
        src1_t[here, :] = source
        return xa, decay1 * xb + source[None]

    unused, s1 = lax.fori_loop(0, LOCAL, middle, (c2, zero), unroll=UNROLL)
    keep[S1] = s1
    begin(s1, vsend, vrecv, vs_sem, vr_sem)

    unused, m1, l01, l11 = near(src1_t, sig1_t, decay1)
    back_step(0, vsend, vrecv, vs_sem, vr_sem, S1, POW1)
    rate1, amp1 = keep[RATE1], keep[AMP1]
    rate2, amp2 = keep[RATE2], keep[AMP2]
    c2 = keep[C2]
    root1 = jnp.sqrt(2.0 * rate1) * SCALE
    half1, turn1 = amp1 * (0.5 * SCALE), amp1 * rate1 * SCALE
    zero_sum = keep[L02] + keep[ZA2] * c2
    one_sum = keep[L12] + keep[ZB2] * c2
    far2 = keep[M2] + (128.0 * keep[POW2 + 2]) * c2
    turn2 = amp2 * rate2 * SCALE
    grads[2] = zero_sum * jnp.sqrt(2.0 * rate2) * SCALE
    grads[3] = amp2 * (0.5 * SCALE) * zero_sum - turn2 * one_sum
    far2 = turn2 * far2
    wait_bytes(yrecv.at[pl.ds(0, 3)], n_sem.at[3])
    y1, y11, y2 = (yrecv[:, k].reshape(STATE) for k in range(3))
    zero_sum = l01 + s1 * y1
    one_sum = l11 + s1 * y11 + m1 * y1
    grads[0] = zero_sum * root1
    grads[1] = half1 * zero_sum - turn1 * one_sum
    grads[3] = grads[3] - far2 * y2

    def share(ref, q):
        return ref.at[q // 4, pl.ds((q % 4) * 2, 2)]

    for i, q in enumerate(plane):
        pltpu.make_async_remote_copy(
            src_ref=share(grads, q), dst_ref=rs_recv.at[i], send_sem=p_send.at[0], recv_sem=p_recv.at[0],
            device_id=(dp, q * 4 + z), device_id_type=MESH,
        ).start()


    back_step(1, vsend, vrecv, vs_sem, vr_sem, S1, POW1)
    wait_bytes(rs_recv, p_recv.at[0])
    total = grads[me // 4, pl.ds((me % 4) * 2, 2)]
    for i in range(15):
        total = total + rs_recv[i]
    zred[z] = total
    for d in (2, 1, 3):
        pltpu.make_async_remote_copy(
            src_ref=zred.at[z], dst_ref=zred.at[z], send_sem=p_send.at[1], recv_sem=p_recv.at[1],
            device_id=at(2, d), device_id_type=MESH,
        ).start()

    outs = (value_out, key1_out, gate1_out, key2_out, gate2_out)

    def store(i, c, tile):
        outs[i][0, c * 128 : (c + 1) * 128, :] = tile.astype(jnp.bfloat16)

    for c in range(4):
        back = back2_t[pl.ds(c, LOCAL, stride=8), :].T
        store(2, c, back * block(2, c) * block(4, c))
        store(3, c, back * (block(3, c) * block(4, c)))
        store(4, c, block(0, c) * block(7, c))


    wait_bytes(zred.at[pl.ds(0, 3)], p_recv.at[1])
    total = (zred[0] + zred[1]) + (zred[2] + zred[3])
    piece[...] = total
    sums_out[me] = total
    for i, q in enumerate(plane):
        pltpu.make_async_remote_copy(
            src_ref=piece, dst_ref=sums_out.at[me], send_sem=p_send.at[2], recv_sem=p_recv.at[2],
            device_id=(dp, q * 4 + z), device_id_type=MESH,
        ).start()

    c1 = back_step(2, vsend, vrecv, vs_sem, vr_sem, S1, POW1)
    decay1 = jnp.exp(-keep[RATE1])
    amp1 = keep[AMP1]

    def last(i, xa):
        t = LOCAL - 1 - i
        xa = decay1 * xa + row(src1_t, t)
        part = jnp.sum(amp1 * xa, axis=0)
        back1_t[pl.ds(pl.multiple_of(t * 8, 8), 8), :] = part + pltpu.roll(part, 4, 0)
        return xa

    lax.fori_loop(0, LOCAL, last, c1, unroll=UNROLL)
    for c in range(4):
        back = back1_t[pl.ds(c, LOCAL, stride=8), :].T
        store(0, c, back * block(5, c))
        store(1, c, back * block(6, c))

    wait_bytes(sums_out.at[pl.ds(0, 15)], p_recv.at[2])
    for axis in range(3):
        for h in range(2):
            departed(axis, urecv, us_sem, h)
            departed(axis, vrecv, vs_sem, h)
    wait_bytes(nrecv.at[pl.ds(0, 3)], n_sem.at[0])
    wait_bytes(yrecv.at[pl.ds(0, 3)], n_sem.at[2])
    for k in range(1, 16):
        @pl.when(me + k < 16)
        def _():
            wait_bytes(tsend, ts_sem.at[k - 1])
    wait_bytes(rs_recv, p_send.at[0])
    wait_bytes(zred.at[pl.ds(0, 3)], p_send.at[1])
    wait_bytes(rs_recv, p_send.at[2])


def hand_over(*refs):
    made, turned, outs, thin, sem = refs[:5], refs[5], refs[6:15], *refs[15:]
    stores = [pltpu.make_async_copy(made[i], outs[i], sem.at[i]) for i in range(5)]
    stores += [pltpu.make_async_copy(thin.at[i], outs[5 + i], sem.at[5 + i]) for i in range(4)]
    for store in stores[:5]:
        store.start()
    for i in range(4):
        for c in range(4):
            thin[i, :, c * 128 : (c + 1) * 128] = turned[pl.ds(i * 64 + c, ORDER, stride=4), :]
        stores[5 + i].start()
    for store in stores:
        store.wait()


def per_device(
    value, key_one, gate_one, conv_one, key_two, gate_two, conv_two, grad_out,
    residues_one, log_rate_one, residues_two, log_rate_two,
):
    f32 = jnp.float32
    vmem = pltpu.VMEM
    dma = pltpu.SemaphoreType.DMA
    turned = vmem((LOCAL * 8, 128), f32)
    bf16 = jnp.bfloat16
    shape = value.shape
    anywhere = pl.BlockSpec(memory_space=pl.ANY)
    inside = pl.BlockSpec(memory_space=pltpu.VMEM)
    made = pl.pallas_call(
        kernel,
        out_shape=[vmem(shape, bf16)] * 5 + [vmem((16, 2, 8, 128), f32)],
        in_specs=[anywhere] * 12,
        out_specs=[inside] * 6,
        scratch_shapes=[
            vmem((8, CHAN, LOCAL), bf16),
            vmem((4, ORDER, CHAN), f32),
            dma((12,)),
            turned, turned, turned, turned, turned, turned, turned,
            vmem((4, 64, 128), f32),
            vmem((19,) + STATE, f32),
            vmem((2, 3, 2) + HALF, f32),
            vmem((2, 3, 3) + HALF, f32),
            vmem((4, 3, 2, 8, 128), f32),
            vmem((4, 3, 2, 8, 128), f32),
            vmem((3, 2, 8, 128), f32),
            vmem((15, 3, 2, 8, 128), f32),
            vmem((4, 3, 2, 8, 128), f32),
            vmem((4, 3, 2, 8, 128), f32),
            vmem((2, 3, 2) + HALF, f32),
            vmem((2, 3, 3) + HALF, f32),
            vmem((4,) + STATE, f32),
            vmem((15, 2, 8, 128), f32),
            vmem((4, 2, 8, 128), f32),
            vmem((2, 8, 128), f32),
            dma((10,)), dma((10,)), dma((4,)), dma((15,)), dma((15,)), dma((10,)), dma((10,)), dma((3,)), dma((3,)),
        ],
        compiler_params=pltpu.CompilerParams(
            collective_id=0, has_side_effects=True, vmem_limit_bytes=56 * 1024 * 1024
        ),
        name="hyena_back",
    )(
        value, key_one, gate_one, conv_one, key_two, gate_two, conv_two, grad_out,
        residues_one.T, log_rate_one.T, residues_two.T, log_rate_two.T,
    )
    made = list(made[:5]) + [made[5].reshape(4 * ORDER * 4, 128)]
    thin = jax.ShapeDtypeStruct((ORDER, CHAN), f32)
    outs = pl.pallas_call(
        hand_over,
        out_shape=[jax.ShapeDtypeStruct(shape, bf16)] * 5 + [thin] * 4,
        in_specs=[inside] * 6,
        out_specs=[anywhere] * 9,
        scratch_shapes=[
            vmem((4, ORDER, CHAN), f32),
            dma((9,)),
        ],
        name="hand_over",
    )(*(pltpu.with_memory_space_constraint(array, pltpu.VMEM) for array in made))
    return tuple(outs[:5]) + tuple(out.T for out in outs[5:])


def solution(mesh):
    wide = P(None, "dp", "context")
    thin = P("dp", None)
    return jax.shard_map(
        per_device,
        mesh=mesh,
        in_specs=(wide,) * 8 + (thin,) * 4,
        out_specs=(wide,) * 5 + (thin,) * 4,
        check_vma=False,
    )
```

```python
import math

import jax
import jax.numpy as jnp
from jax import lax
from jax.experimental import pallas as pl
from jax.experimental.pallas import tpu as pltpu
from jax.sharding import PartitionSpec as P

MESH = pl.DeviceIdType.MESH
LOCAL = 128
CHAN = 512
ORDER = 16
STATE = (8, 8, 128)
HALF = (4, 8, 128)
SCALE = 1.0 / math.sqrt(8192.0)
UNROLL = 16

(AMP1, RATE1, AMP2, RATE2, S2, M2, L02, L12, ZA2, ZB2, C2, S1, EU, POW1, POW2) = (*range(13), 13, 16)


def wait_bytes(ref, sem):
    pltpu.make_async_copy(ref, ref, sem).wait()


def kernel(
    value, key_one, gate_one, conv_one, key_two, gate_two, conv_two, grad_out, res1, lr1, res2, lr2,
    value_out, key1_out, gate1_out, key2_out, gate2_out, sums_out,
    wide, narrow, in_sem, src2_t, gain_t, sig1_t, sig2_t, src1_t, back2_t, back1_t, par,
    keep, usend, urecv, nsend, nrecv, tsend, trecv, ysend, yrecv, vsend, vrecv, grads, rs_recv, zred, piece,
    us_sem, ur_sem, n_sem, ts_sem, tr_sem, vs_sem, vr_sem, p_send, p_recv,
):
    dp = lax.axis_index("dp")
    ctx = lax.axis_index("context")
    y, x, z = ctx // 16, (ctx // 4) % 4, ctx % 4
    me = ctx // 4
    coords = (y, x, z)

    def at(axis, d):
        if axis == 0:
            return (dp, ((y + d) % 4) * 16 + x * 4 + z)
        if axis == 1:
            return (dp, y * 16 + ((x + d) % 4) * 4 + z)
        return (dp, y * 16 + x * 4 + (z + d) % 4)

    plane = [
        (((y + e) % 4) * 4 + (x + f) % 4) for e in (2, 1, 3, 0) for f in (2, 1, 3, 0) if e or f
    ]

    barrier = pltpu.get_barrier_semaphore()
    for d in (2, 1, 3):
        pl.semaphore_signal(barrier, inc=1, device_id=at(2, d), device_id_type=MESH)

    trecv[...] = jnp.zeros(trecv.shape, jnp.float32)
    for h in range(2):
        urecv[h, 0] = jnp.zeros(urecv.shape[2:], jnp.float32)
        vrecv[h, 0] = jnp.zeros(vrecv.shape[2:], jnp.float32)

    for axis in (0, 1):
        for d in (2, 1, 3):
            pl.semaphore_signal(barrier, inc=1, device_id=at(axis, d), device_id_type=MESH)

    wide_in = (grad_out, gate_two, key_two, gate_one, conv_one, key_one, value, conv_two)
    narrow_in = (lr2, lr1, res2, res1)
    loads = []
    for i, ref in enumerate(narrow_in):
        loads.append(pltpu.make_async_copy(ref, narrow.at[i], in_sem.at[8 + i]))
    for i, ref in enumerate(wide_in):
        loads.append(pltpu.make_async_copy(ref.at[0], wide.at[i], in_sem.at[i]))
    for load in loads:
        load.start()

    for i in range(4):
        loads[i].wait()
        for c in range(4):
            par[i, pl.ds(c, ORDER, stride=4), :] = narrow[i, :, c * 128 : (c + 1) * 128]
    rate2 = jnp.exp(par[0]).reshape(STATE)
    rate1 = jnp.exp(par[1]).reshape(STATE)
    keep[RATE2] = rate2
    keep[RATE1] = rate1
    keep[AMP2] = par[2].reshape(STATE) * jnp.sqrt(2.0 * rate2)
    keep[AMP1] = par[3].reshape(STATE) * jnp.sqrt(2.0 * rate1)

    def block(i, c):
        return wide[i, c * 128 : (c + 1) * 128, :].astype(jnp.float32)

    def put(ref, c, tile):
        flipped = tile.T
        ref[pl.ds(c, LOCAL, stride=8), :] = flipped
        ref[pl.ds(c + 4, LOCAL, stride=8), :] = flipped

    def row(ref, t):
        return ref[pl.ds(pl.multiple_of(t * 8, 8), 8), :][None]

    zero = jnp.zeros(STATE, jnp.float32)

    loads[4].wait()
    loads[5].wait()
    for c in range(4):
        put(src2_t, c, block(0, c) * block(1, c))

    decay2 = jnp.exp(-rate2)

    def first(i, state):
        return decay2 * state + row(src2_t, LOCAL - 1 - i)

    state = lax.fori_loop(0, LOCAL, first, zero, unroll=UNROLL)
    keep[S2] = state

    for i in range(6, 12):
        loads[i].wait()
    for c in range(4):
        kt, go = block(2, c), block(3, c)
        put(gain_t, c, kt * go)
        put(sig2_t, c, kt * (go * block(4, c)))
        put(sig1_t, c, block(5, c) * block(6, c))

    decay1 = jnp.exp(-keep[RATE1])

    def ahead(t, st):
        a0, a1, b0, b1 = st
        u = a0 + row(sig1_t, t)
        v = b0 + row(sig2_t, t)
        return decay1 * u, decay1 * (a1 + u), decay2 * v, decay2 * (b1 + v)

    za1, zb1, za2, zb2 = lax.fori_loop(0, LOCAL, ahead, (zero,) * 4, unroll=UNROLL)
    keep[ZA2], keep[ZB2] = za2, zb2
    for k, array in enumerate((za1, zb1, za2)):
        nsend[:, k] = array.reshape(4, 2, 8, 128)

    pl.semaphore_wait(barrier, 9)

    def send(axis, buf, recv, ssem, rsem, h):
        for d in (2, 1, 3):
            copy = pltpu.make_async_remote_copy(
                src_ref=buf.at[h, axis, 0 if axis == 0 else (coords[axis] + d) // 4],
                dst_ref=recv.at[h, axis, 3 - d],
                send_sem=ssem.at[5 * h + (d - 1 if axis == 0 else axis + 2)],
                recv_sem=rsem.at[5 * h + (3 - d if axis == 0 else axis + 2)],
                device_id=at(axis, d),
                device_id_type=MESH,
            )
            if axis:
                copy.start()
            else:
                pl.when(y + d >= 4)(copy.start)

    def arrived(axis, recv, rsem, h):
        if axis:
            wait_bytes(recv.at[h, axis], rsem.at[5 * h + axis + 2])
        else:
            for d in (1, 2, 3):
                @pl.when(y + d < 4)
                def _():
                    wait_bytes(recv.at[h, 0, d - 1], rsem.at[5 * h + d - 1])

    def departed(axis, recv, ssem, h):
        if axis:
            wait_bytes(recv.at[h, axis], ssem.at[5 * h + axis + 2])
        else:
            for d in (1, 2, 3):
                @pl.when(y + d >= 4)
                def _():
                    wait_bytes(recv.at[h, 0, d - 1], ssem.at[5 * h + d - 1])

    strides = (2048.0, 512.0, 128.0)

    def spread_signals():
        for d in (2, 1, 3):
            pltpu.make_async_remote_copy(
                src_ref=nsend.at[(z + d) % 4], dst_ref=nrecv.at[z], send_sem=n_sem.at[0], recv_sem=n_sem.at[1],
                device_id=at(2, d), device_id_type=MESH,
            ).start()
        nrecv[z] = nsend[z]

    def quarter_rates():
        return keep[RATE1, pl.ds(2 * z, 2)], keep[RATE2, pl.ds(2 * z, 2)]

    def shifted(state, length, powers):
        f0, f1, f2 = state
        return powers[0] * f0, powers[0] * (f1 + length * f0), powers[1] * f2

    def added(left, right):
        return tuple(p + q for p, q in zip(left, right))

    def line(i):
        return tuple(nrecv[i, k] for k in range(3))

    def total_lines():
        wait_bytes(nrecv.at[pl.ds(0, 3)], n_sem.at[1])
        powers = tuple(jnp.exp(-128.0 * rate) for rate in quarter_rates())
        state = line(0)
        for i in (1, 2, 3):
            state = added(line(i), shifted(state, 128.0, powers))
        for k in range(3):
            tsend[k] = state[k]
        for k in (10, 6, 9, 14, 11, 7, 5, 13, 2, 8, 3, 15, 4, 1, 12):
            @pl.when(me + k < 16)
            def _():
                pltpu.make_async_remote_copy(
                    src_ref=tsend, dst_ref=trecv.at[k - 1], send_sem=ts_sem.at[k - 1], recv_sem=tr_sem.at[k - 1],
                    device_id=(dp, (me + k) * 4 + z), device_id_type=MESH,
                ).start()


    def return_signals():
        near_powers = []
        powers = []
        for rate in quarter_rates():
            powers.append(jnp.exp(-512.0 * rate))
            near_powers.append(jnp.exp(-128.0 * rate))
        for k in range(1, 16):
            @pl.when(me >= k)
            def _():
                wait_bytes(trecv.at[k - 1], tr_sem.at[k - 1])
        state = tuple(jnp.zeros((2, 8, 128), jnp.float32) for _ in range(3))
        for k in range(15, 0, -1):
            block = tuple(trecv[k - 1, i] for i in range(3))
            state = added(block, shifted(state, 512.0, powers))
        for i in range(4):
            for k in range(3):
                ysend[i, k] = state[k]
            state = added(line(i), shifted(state, 128.0, near_powers))
        for d in (2, 1, 3):
            pltpu.make_async_remote_copy(
                src_ref=ysend.at[(z + d) % 4], dst_ref=yrecv.at[z], send_sem=n_sem.at[2], recv_sem=n_sem.at[3],
                device_id=at(2, d), device_id_type=MESH,
            ).start()
        yrecv[z] = ysend[z]

    def back_step(axis, buf, recv, ssem, rsem, own, power):
        for h in range(2):
            part = pl.ds(4 * h, 4)
            arrived(axis, recv, rsem, h)
            scale = keep[power + axis, part]
            far = recv[h, axis, 2]
            if axis:
                far = far + scale * keep[EU, part]
            for d in (2, 1):
                far = recv[h, axis, d - 1] + scale * far
            keep[EU, part] = far
            if axis < 2:
                buf[h, axis + 1, 0] = far
                buf[h, axis + 1, 1] = keep[own, part] + scale * far
                send(axis + 1, buf, recv, ssem, rsem, h)
        return keep[EU]

    def begin(state, buf, recv, ssem, rsem):
        for h in range(2):
            buf[h, 0, 0] = state[4 * h : 4 * h + 4]
            send(0, buf, recv, ssem, rsem, h)

    spread_signals()
    begin(keep[S2], usend, urecv, us_sem, ur_sem)

    for axis, step in enumerate(strides):
        keep[POW2 + axis] = jnp.exp(-step * rate2)
        keep[POW1 + axis] = jnp.exp(-step * keep[RATE1])

    def near(src_t, sig_t, decay):
        def body(i, st):
            t = LOCAL - 1 - i
            x0, x1, l0, l1 = st
            x1 = decay * (x1 + x0)
            x0 = decay * x0 + row(src_t, t)
            sig = row(sig_t, t)
            return x0, x1, l0 + sig * x0, l1 + sig * x1

        return lax.fori_loop(0, LOCAL, body, (zero,) * 4, unroll=UNROLL)

    unused, m2, l02, l12 = near(src2_t, sig2_t, decay2)
    keep[M2], keep[L02], keep[L12] = m2, l02, l12

    back_step(0, usend, urecv, us_sem, ur_sem, S2, POW2)
    back_step(1, usend, urecv, us_sem, ur_sem, S2, POW2)
    total_lines()
    return_signals()
    c2 = back_step(2, usend, urecv, us_sem, ur_sem, S2, POW2)
    keep[C2] = c2

    decay1 = jnp.exp(-keep[RATE1])
    decay2 = jnp.exp(-keep[RATE2])
    amp2 = keep[AMP2]

    def middle(i, st):
        t = LOCAL - 1 - i
        xa, xb = st
        xa = decay2 * xa + row(src2_t, t)
        part = jnp.sum(amp2 * xa, axis=0)
        back = part + pltpu.roll(part, 4, 0)
        here = pl.ds(pl.multiple_of(t * 8, 8), 8)
        back2_t[here, :] = back
        source = back * gain_t[here, :]
        src1_t[here, :] = source
        return xa, decay1 * xb + source[None]

    unused, s1 = lax.fori_loop(0, LOCAL, middle, (c2, zero), unroll=UNROLL)
    keep[S1] = s1
    begin(s1, vsend, vrecv, vs_sem, vr_sem)

    unused, m1, l01, l11 = near(src1_t, sig1_t, decay1)
    back_step(0, vsend, vrecv, vs_sem, vr_sem, S1, POW1)
    rate1, amp1 = keep[RATE1], keep[AMP1]
    rate2, amp2 = keep[RATE2], keep[AMP2]
    c2 = keep[C2]
    root1 = jnp.sqrt(2.0 * rate1) * SCALE
    half1, turn1 = amp1 * (0.5 * SCALE), amp1 * rate1 * SCALE
    zero_sum = keep[L02] + keep[ZA2] * c2
    one_sum = keep[L12] + keep[ZB2] * c2
    far2 = keep[M2] + (128.0 * keep[POW2 + 2]) * c2
    turn2 = amp2 * rate2 * SCALE
    grads[2] = zero_sum * jnp.sqrt(2.0 * rate2) * SCALE
    grads[3] = amp2 * (0.5 * SCALE) * zero_sum - turn2 * one_sum
    far2 = turn2 * far2
    wait_bytes(yrecv.at[pl.ds(0, 3)], n_sem.at[3])
    y1, y11, y2 = (yrecv[:, k].reshape(STATE) for k in range(3))
    zero_sum = l01 + s1 * y1
    one_sum = l11 + s1 * y11 + m1 * y1
    grads[0] = zero_sum * root1
    grads[1] = half1 * zero_sum - turn1 * one_sum
    grads[3] = grads[3] - far2 * y2

    def share(ref, q):
        return ref.at[q // 4, pl.ds((q % 4) * 2, 2)]

    for i, q in enumerate(plane):
        pltpu.make_async_remote_copy(
            src_ref=share(grads, q), dst_ref=rs_recv.at[i], send_sem=p_send.at[0], recv_sem=p_recv.at[0],
            device_id=(dp, q * 4 + z), device_id_type=MESH,
        ).start()


    back_step(1, vsend, vrecv, vs_sem, vr_sem, S1, POW1)
    wait_bytes(rs_recv, p_recv.at[0])
    total = grads[me // 4, pl.ds((me % 4) * 2, 2)]
    for i in range(15):
        total = total + rs_recv[i]
    zred[z] = total
    for d in (2, 1, 3):
        pltpu.make_async_remote_copy(
            src_ref=zred.at[z], dst_ref=zred.at[z], send_sem=p_send.at[1], recv_sem=p_recv.at[1],
            device_id=at(2, d), device_id_type=MESH,
        ).start()

    outs = (value_out, key1_out, gate1_out, key2_out, gate2_out)

    def store(i, c, tile):
        outs[i][0, c * 128 : (c + 1) * 128, :] = tile.astype(jnp.bfloat16)

    for c in range(4):
        back = back2_t[pl.ds(c, LOCAL, stride=8), :].T
        store(2, c, back * block(2, c) * block(4, c))
        store(3, c, back * (block(3, c) * block(4, c)))
        store(4, c, block(0, c) * block(7, c))


    wait_bytes(zred.at[pl.ds(0, 3)], p_recv.at[1])
    total = (zred[0] + zred[1]) + (zred[2] + zred[3])
    piece[...] = total
    sums_out[me] = total
    for i, q in enumerate(plane):
        pltpu.make_async_remote_copy(
            src_ref=piece, dst_ref=sums_out.at[me], send_sem=p_send.at[2], recv_sem=p_recv.at[2],
            device_id=(dp, q * 4 + z), device_id_type=MESH,
        ).start()

    c1 = back_step(2, vsend, vrecv, vs_sem, vr_sem, S1, POW1)
    decay1 = jnp.exp(-keep[RATE1])
    amp1 = keep[AMP1]

    def last(i, xa):
        t = LOCAL - 1 - i
        xa = decay1 * xa + row(src1_t, t)
        part = jnp.sum(amp1 * xa, axis=0)
        back1_t[pl.ds(pl.multiple_of(t * 8, 8), 8), :] = part + pltpu.roll(part, 4, 0)
        return xa

    lax.fori_loop(0, LOCAL, last, c1, unroll=UNROLL)
    for c in range(4):
        back = back1_t[pl.ds(c, LOCAL, stride=8), :].T
        store(0, c, back * block(5, c))
        store(1, c, back * block(6, c))

    wait_bytes(sums_out.at[pl.ds(0, 15)], p_recv.at[2])
    for axis in range(3):
        for h in range(2):
            departed(axis, urecv, us_sem, h)
            departed(axis, vrecv, vs_sem, h)
    wait_bytes(nrecv.at[pl.ds(0, 3)], n_sem.at[0])
    wait_bytes(yrecv.at[pl.ds(0, 3)], n_sem.at[2])
    for k in range(1, 16):
        @pl.when(me + k < 16)
        def _():
            wait_bytes(tsend, ts_sem.at[k - 1])
    wait_bytes(rs_recv, p_send.at[0])
    wait_bytes(zred.at[pl.ds(0, 3)], p_send.at[1])
    wait_bytes(rs_recv, p_send.at[2])


def hand_over(*refs):
    made, turned, outs, thin, sem = refs[:5], refs[5], refs[6:15], *refs[15:]
    stores = [pltpu.make_async_copy(made[i], outs[i], sem.at[i]) for i in range(5)]
    stores += [pltpu.make_async_copy(thin.at[i], outs[5 + i], sem.at[5 + i]) for i in range(4)]
    for store in stores[:5]:
        store.start()
    for i in range(4):
        for c in range(4):
            thin[i, :, c * 128 : (c + 1) * 128] = turned[pl.ds(i * 64 + c, ORDER, stride=4), :]
        stores[5 + i].start()
    for store in stores:
        store.wait()


def per_device(
    value, key_one, gate_one, conv_one, key_two, gate_two, conv_two, grad_out,
    residues_one, log_rate_one, residues_two, log_rate_two,
):
    f32 = jnp.float32
    vmem = pltpu.VMEM
    dma = pltpu.SemaphoreType.DMA
    turned = vmem((LOCAL * 8, 128), f32)
    bf16 = jnp.bfloat16
    shape = value.shape
    anywhere = pl.BlockSpec(memory_space=pl.ANY)
    inside = pl.BlockSpec(memory_space=pltpu.VMEM)
    made = pl.pallas_call(
        kernel,
        out_shape=[vmem(shape, bf16)] * 5 + [vmem((16, 2, 8, 128), f32)],
        in_specs=[anywhere] * 12,
        out_specs=[inside] * 6,
        scratch_shapes=[
            vmem((8, CHAN, LOCAL), bf16),
            vmem((4, ORDER, CHAN), f32),
            dma((12,)),
            turned, turned, turned, turned, turned, turned, turned,
            vmem((4, 64, 128), f32),
            vmem((19,) + STATE, f32),
            vmem((2, 3, 2) + HALF, f32),
            vmem((2, 3, 3) + HALF, f32),
            vmem((4, 3, 2, 8, 128), f32),
            vmem((4, 3, 2, 8, 128), f32),
            vmem((3, 2, 8, 128), f32),
            vmem((15, 3, 2, 8, 128), f32),
            vmem((4, 3, 2, 8, 128), f32),
            vmem((4, 3, 2, 8, 128), f32),
            vmem((2, 3, 2) + HALF, f32),
            vmem((2, 3, 3) + HALF, f32),
            vmem((4,) + STATE, f32),
            vmem((15, 2, 8, 128), f32),
            vmem((4, 2, 8, 128), f32),
            vmem((2, 8, 128), f32),
            dma((10,)), dma((10,)), dma((4,)), dma((15,)), dma((15,)), dma((10,)), dma((10,)), dma((3,)), dma((3,)),
        ],
        compiler_params=pltpu.CompilerParams(
            collective_id=0, has_side_effects=True, vmem_limit_bytes=56 * 1024 * 1024
        ),
        name="hyena_back",
    )(
        value, key_one, gate_one, conv_one, key_two, gate_two, conv_two, grad_out,
        residues_one.T, log_rate_one.T, residues_two.T, log_rate_two.T,
    )
    made = list(made[:5]) + [made[5].reshape(4 * ORDER * 4, 128)]
    thin = jax.ShapeDtypeStruct((ORDER, CHAN), f32)
    outs = pl.pallas_call(
        hand_over,
        out_shape=[jax.ShapeDtypeStruct(shape, bf16)] * 5 + [thin] * 4,
        in_specs=[inside] * 6,
        out_specs=[anywhere] * 9,
        scratch_shapes=[
            vmem((4, ORDER, CHAN), f32),
            dma((9,)),
        ],
        name="hand_over",
    )(*(pltpu.with_memory_space_constraint(array, pltpu.VMEM) for array in made))
    return tuple(outs[:5]) + tuple(out.T for out in outs[5:])


def solution(mesh):
    wide = P(None, "dp", "context")
    thin = P("dp", None)
    return jax.shard_map(
        per_device,
        mesh=mesh,
        in_specs=(wide,) * 8 + (thin,) * 4,
        out_specs=(wide,) * 5 + (thin,) * 4,
        check_vma=False,
    )
```
